32 devices in a mesh: grp: 2 (over y), space: 4 (over z), cuts: 2 (over x), sub: 2 (over core).
Axes of the slice: x: 2, y: 2, z: 4, core: 2. Of those that a mesh axis runs over, the one named last changes fastest.
Arguments:
- starts: float32 [16, 2, 256, 512], P(('grp', 'cuts'), None, ('space', 'sub')), parts along dimension 0, may hold values from -6 to 6
- coarse_prev: float32 [16, 2, 64, 128], P(('grp', 'cuts'), None, ('space', 'sub')), parts along dimension 0, may hold values from -6 to 6
- zone_ids: int32 [512, 512], P(('grp', 'space', 'sub')), parts along dimension 0, may hold values from 0 to 7
- materials: float32 [4, 8], replicated, may hold values from 0.05 to 0.2
- current: int32 [192], P('grp'), parts along dimension 0, may hold values from 0 to 1999
- bounds: int32 [8], replicated, may hold values from 0 to 94
Outputs:
- ends: float32 [16, 2, 256, 512], P(('grp', 'cuts'), None, ('space', 'sub')), parts along dimension 0
- coarse_new: float32 [16, 2, 64, 128], P(('grp', 'cuts'), None, ('space', 'sub')), parts along dimension 0
The draws below stay inside these ranges and needn't reach their ends.
There are 2 independent parts, one for each index of `grp`. The reference program is written for one: setup_inputs(seed, part) draws one part's arguments, and reference() takes and returns one part's arrays. A program takes and returns all parts, laid end to end along the dimension named above; an argument that names none is the same for every part. Nothing has to cross between parts.
All inputs are finite; a program needn't handle non-finite values.
Results may differ from the reference program's by a relative error of at most 0.0001.
Values sent between devices are 32-bit elements; how exact they have to be, the bound alone decides.
A program may use at most 64 MiB of HBM per device.

```python
import math
import jax
import jax.numpy as jnp

NY = 512
SLICES = 8
FSTEPS = 2
PROFILE = 96
ZONES = 8
NX = 256
NXC = 64
NYC = 128


def draw_bounds(key, part):
    window = PROFILE // SLICES
    offsets = jax.random.randint(key, (SLICES,), 0, window - FSTEPS + 1)
    position = jnp.arange(SLICES)
    offsets = jnp.where(position == 0, 0, jnp.where(position == SLICES - 1, window - FSTEPS, offsets))
    return (position * window + offsets).astype(jnp.int32)


def place_ends(drawn, own_key, smallest, top_value):
    longest = drawn.shape.index(max(drawn.shape))
    spots = []
    for shift in (0, 1):
        where = [jax.random.randint(jax.random.fold_in(own_key, axis), (), 0, length) for axis, length in enumerate(drawn.shape)]
        where[longest] = (where[longest] + shift) % drawn.shape[longest]
        spots.append(tuple(where))
    return drawn.at[spots[0]].set(smallest).at[spots[1]].set(top_value)


def block_scale(key, dims, split, least, high):
    def one(axis_at, blocks):
        draws = jax.random.uniform(jax.random.fold_in(jax.random.fold_in(key, 6), axis_at), (blocks,), jnp.float32, least / len(split), high / len(split))
        return jnp.repeat(jnp.exp(draws), dims[axis_at] // blocks).reshape((-1,) + (1,) * (len(dims) - axis_at - 1))

    gain = one(*split[0])
    for cut in split[1:]:
        gain = gain * one(*cut)
    return gain


def scatter_about(stream_key, dims, width, reach, shards=(), held_as=jnp.bfloat16):
    array = width * jax.random.normal(stream_key, dims, jnp.float32)
    if shards:
        array = array * block_scale(stream_key, dims, shards, -0.22, 0.18)
    return jnp.clip(array, -reach, reach).astype(held_as)


def setup_inputs(seed: int = 0, part: int = 0) -> dict:
    key_of = jax.random.split(jax.random.key(seed), 7)
    part_keys = jax.random.split(jax.random.fold_in(key_of[6], part), 7)
    return {
        "starts": scatter_about(part_keys[0], (SLICES, 2, NX, NY), 1.0, 6.0, ((0, 2), (2, 8)), jnp.float32),
        "coarse_prev": scatter_about(part_keys[1], (SLICES, 2, NXC, NYC), 1.0, 6.0, ((0, 2), (2, 8)), jnp.float32),
        "zone_ids": place_ends(jax.random.randint(part_keys[2], (NX, NY), 0, ZONES), jax.random.fold_in(part_keys[2], 1), 0, ZONES - 1).astype(jnp.int32),
        "materials": jnp.clip(jnp.exp(jax.random.uniform(key_of[3], (4, ZONES), jnp.float32, math.log(0.05), math.log(0.2))), 0.05, 0.2),
        "current": place_ends(jax.random.randint(part_keys[4], (PROFILE,), 0, 2000), jax.random.fold_in(part_keys[4], 1), 0, 1999).astype(jnp.int32),
        "bounds": draw_bounds(jax.random.fold_in(key_of[6], 71), part),
    }


JOULE_GAIN = 0.5


def restrict(values):
    shape = values.shape
    blocks = values.reshape(shape[:-2] + (shape[-2] // 4, 4, shape[-1] // 4, 4))
    return jnp.mean(blocks, axis=(-3, -1))


def prolong(coarse):
    return jnp.repeat(jnp.repeat(coarse, 4, axis=-2), 4, axis=-1)


def material_fields(zone_pad, materials):
    fields = jnp.zeros((4,) + zone_pad.shape, jnp.float32)
    for zone_no in range(materials.shape[1]):
        present = (zone_pad == zone_no)[None]
        fields = jnp.where(present, materials[:, zone_no][:, None, None], fields)
    return fields


def stencil(padded, diffusion):
    center = padded[:, 1:-1, 1:-1]
    own = diffusion[:, 1:-1, 1:-1]
    summed = 0.5 * (diffusion[:, 2:, 1:-1] + own) * (padded[:, 2:, 1:-1] - center)
    summed = summed + 0.5 * (diffusion[:, :-2, 1:-1] + own) * (padded[:, :-2, 1:-1] - center)
    summed = summed + 0.5 * (diffusion[:, 1:-1, 2:] + own) * (padded[:, 1:-1, 2:] - center)
    summed = summed + 0.5 * (diffusion[:, 1:-1, :-2] + own) * (padded[:, 1:-1, :-2] - center)
    return summed


def advance(padded, diffusion, coupling, turns, amperes, time_span):
    center = padded[:, 1:-1, 1:-1]
    spread = stencil(padded, diffusion)
    change = spread[0] + time_span * turns * amperes
    magnet = center[0] + change
    thermal = center[1] + spread[1] + JOULE_GAIN * change * change
    coupled = time_span * coupling
    diagonal = 1.0 + coupled
    offdiag = 0.5 * coupled
    determinant = diagonal * diagonal - offdiag * offdiag
    return jnp.stack([(diagonal * magnet + offdiag * thermal) / determinant,
                      (offdiag * magnet + diagonal * thermal) / determinant])


def reference(starts, coarse_prev, zone_ids, materials, current, bounds):
    zone_pad = jnp.pad(zone_ids, 4)
    fields = material_fields(zone_pad, materials)
    fine_diff = fields[0:2, 3:-3, 3:-3]
    fine_link = fields[2, 4:-4, 4:-4]
    fine_turn = fields[3, 4:-4, 4:-4]
    coarse_fields = restrict(fields)
    coarse_diff = coarse_fields[0:2] * 0.125
    coarse_link = coarse_fields[2, 1:-1, 1:-1]
    coarse_turn = coarse_fields[3, 1:-1, 1:-1]
    amperes_all = current.astype(jnp.float32) * 0.001
    corrections = []
    for slice_no in range(SLICES):
        state = starts[slice_no]
        for step_no in range(FSTEPS):
            padded = jnp.pad(state, ((0, 0), (1, 1), (1, 1)))
            state = advance(padded, fine_diff, fine_link, fine_turn,
                            amperes_all[bounds[slice_no] + step_no], 1.0)
        corrections.append(state - prolong(coarse_prev[slice_no]))
    coarse_state = restrict(starts[0])
    ends = []
    coarse_outs = []
    for slice_no in range(SLICES):
        padded = jnp.pad(coarse_state, ((0, 0), (1, 1), (1, 1)))
        coarse_out = advance(padded, coarse_diff, coarse_link, coarse_turn,
                             amperes_all[bounds[slice_no]], 2.0)
        coarse_outs.append(coarse_out)
        ends.append(prolong(coarse_out) + corrections[slice_no])
        coarse_state = coarse_out + restrict(corrections[slice_no])
    return (jnp.stack(ends), jnp.stack(coarse_outs))
```

```python
import functools
import jax
import jax.numpy as jnp
from jax import lax
from jax.experimental import pallas as pl
from jax.experimental.pallas import tpu as pltpu
from jax.sharding import PartitionSpec as P

JOULE_GAIN = 0.5
MESH = pl.DeviceIdType.MESH
F32 = jnp.float32
BF16 = jnp.bfloat16


def pieces(values):
    high = values.astype(BF16)
    low = (values - high.astype(F32)).astype(BF16)
    return jnp.concatenate([high, low], axis=1)


def advance(sums, turn_amps, keep, mix):
    change = sums[0][1] + turn_amps
    magnet = sums[0][0] + change
    thermal = sums[1][0] + sums[1][1] + JOULE_GAIN * change * change
    return keep * magnet + mix * thermal, mix * magnet + keep * thermal


def link_factors(coupling, span):
    coupled = span * coupling
    diagonal = 1.0 + coupled
    offdiag = 0.5 * coupled
    determinant = diagonal * diagonal - offdiag * offdiag
    return diagonal / determinant, offdiag / determinant


def kernel(
    sizes, starts_hbm, prev_ref, zone_ref, mat_ref, current_ref, bounds_ref,
    gather_ref, spread_ref, ends_ref, new_ref,
    s0, s1, rf, fl, wt, pqs, zt, zb, mu, md, ht, hb, cf, grid_c, tbuf, pbuf, ybuf,
    in_sem, out_sem, send_near, recv_near, send_c, recv_c,
):
    cuts, nsub, tiles, lc, rows, cols, zones, half = sizes
    crow, ccol = rows // 4, cols // 4
    chunks = rows // 8
    cut = lax.axis_index("cuts")
    tile = lax.axis_index("space") * nsub + lax.axis_index("sub")
    has_up = tile > 0
    has_down = tile < tiles - 1
    base = cut * lc

    def where_is(side, cut_no=None):
        other = tile + (side - 1)
        place = {"space": lax.div(other, nsub), "sub": lax.rem(other, nsub)}
        if cut_no is not None:
            place["cuts"] = cut_no
        return place

    def on_side(side):
        if side == 1:
            return lambda fn: fn()
        return pl.when(has_up if side == 0 else has_down)

    load = pltpu.make_async_copy(starts_hbm, s0.at[:, :, pl.ds(8, rows), :], in_sem.at[0])
    load.start()

    barrier = pltpu.get_barrier_semaphore()
    for side in (0, 2):
        @on_side(side)
        def _():
            pl.semaphore_signal(barrier, inc=1, device_id=where_is(side), device_id_type=MESH)
    for step in range(1, cuts):
        other_cut = lax.rem(cut + step, cuts)
        for side in range(3):
            @on_side(side)
            def _():
                pl.semaphore_signal(
                    barrier, inc=1, device_id=where_is(side, other_cut), device_id_type=MESH
                )

    row8 = lax.broadcasted_iota(jnp.int32, (8, cols), 0)
    col8 = lax.broadcasted_iota(jnp.int32, (8, cols), 1)
    rowh = lax.broadcasted_iota(jnp.int32, (2 * half, cols), 0)
    colh = lax.broadcasted_iota(jnp.int32, (2 * half, cols), 1)

    def lookup(zone):
        found = [jnp.full(zone.shape, mat_ref[m, 0], F32) for m in range(4)]
        for zone_no in range(1, zones):
            present = zone == zone_no
            found = [jnp.where(present, mat_ref[m, zone_no], found[m]) for m in range(4)]
        return found

    def restricted(values, buf):
        count = values.shape[0]
        buf[0:count, :] = jnp.dot(
            pieces(values), gather_ref[...], preferred_element_type=F32
        )
        total = buf[pl.ds(0, count // 4, stride=4), :]
        for part in range(1, 4):
            total = total + buf[pl.ds(part, count // 4, stride=4), :]
        return total

    for i in range(chunks):
        found = lookup(zone_ref[8 * i : 8 * i + 8, :])
        for m in range(4):
            fl[m, 8 * i : 8 * i + 8, :] = found[m]
        for m in range(2):
            rf[m, 8 + 8 * i : 16 + 8 * i, :] = found[m]
        keep, mix = link_factors(found[2], 1.0)
        pqs[0, 8 * i : 8 * i + 8, :] = keep
        pqs[1, 8 * i : 8 * i + 8, :] = mix
        pqs[2, 8 * i : 8 * i + 8, :] = found[3]

    load.wait()
    if lc < half:
        mu[...] = jnp.zeros(mu.shape, F32)
        md[...] = jnp.zeros(md.shape, F32)
    for n in range(lc):
        for m in range(2):
            mu[m, half + n : half + n + 1, :] = s0[n, m, 8:9, :]
            mu[m, n : n + 1, :] = s0[n, m, 9:10, :]
            md[m, n : n + 1, :] = s0[n, m, rows + 7 : rows + 8, :]
            md[m, half + n : half + n + 1, :] = s0[n, m, rows + 6 : rows + 7, :]

    ups = jnp.where(has_up, 1, 0) + jnp.where(has_down, 1, 0)
    pl.semaphore_wait(barrier, ups + (cuts - 1) * (1 + ups))

    def near(what, side):
        if what == 0:
            source = zone_ref.at[0:8] if side == 0 else zone_ref.at[rows - 8 : rows]
            target = zb if side == 0 else zt
        elif what == 1:
            source = mu if side == 0 else md
            target = hb if side == 0 else ht
        else:
            source = cf.at[:, pl.ds(crow, crow), :]
            target = cf.at[:, pl.ds(2 * crow if side == 0 else 0, crow), :]
        return pltpu.make_async_remote_copy(
            src_ref=source,
            dst_ref=target,
            send_sem=send_near.at[what, side // 2],
            recv_sem=recv_near.at[what, side // 2],
            device_id=where_is(side),
            device_id_type=MESH,
        )

    def coarse_copy(side, g, local_no, dest):
        return pltpu.make_async_remote_copy(
            src_ref=grid_c.at[g, :, pl.ds(crow, crow), :],
            dst_ref=grid_c.at[g, :, pl.ds((2 - side) * crow, crow), :],
            send_sem=send_c.at[dest, side, local_no],
            recv_sem=recv_c.at[2 - side, g],
            device_id=where_is(side, None if dest == 0 else dest),
            device_id_type=MESH,
        )

    def each_coarse_send(g, local_no, nearby, action):
        for dest in range(1, cuts):
            @pl.when(cut < dest)
            def _():
                for side in (1, 0, 2):
                    @on_side(side)
                    def _():
                        action(coarse_copy(side, g, local_no, dest))
        if nearby:
            for side in (0, 2):
                @on_side(side)
                def _():
                    action(coarse_copy(side, g, local_no, 0))

    def await_coarse(side, g):
        pltpu.make_async_remote_copy(
            src_ref=grid_c.at[g, :, pl.ds(crow, crow), :],
            dst_ref=grid_c.at[g, :, pl.ds(side * crow, crow), :],
            send_sem=send_c.at[0, 0, 0],
            recv_sem=recv_c.at[side, g],
            device_id=where_is(1, lax.rem(cut + 1, cuts)),
            device_id_type=MESH,
        ).wait_recv()

    for what in (0, 1):
        for side in (0, 2):
            @on_side(side)
            def _():
                near(what, side).start()

    @pl.when(jnp.logical_not(has_up))
    def _():
        zt[...] = jnp.zeros(zt.shape, jnp.int32)
        ht[...] = jnp.zeros(ht.shape, F32)
        for m in range(4):
            cf[m, 0:crow, :] = jnp.full((crow, ccol), mat_ref[m, 0], F32)
        grid_c[:, :, 0:crow, :] = jnp.zeros(grid_c.shape[:2] + (crow, ccol), F32)

    @pl.when(jnp.logical_not(has_down))
    def _():
        zb[...] = jnp.zeros(zb.shape, jnp.int32)
        hb[...] = jnp.zeros(hb.shape, F32)
        for m in range(4):
            cf[m, 2 * crow : 3 * crow, :] = jnp.full((crow, ccol), mat_ref[m, 0], F32)
        grid_c[:, :, 2 * crow : 3 * crow, :] = jnp.zeros(grid_c.shape[:2] + (crow, ccol), F32)

    own_c = restricted(fl[...].reshape(4 * rows, cols), tbuf)
    for m in range(4):
        cf[m, crow : 2 * crow, :] = own_c[m * crow : (m + 1) * crow]
    for side in (0, 2):
        @on_side(side)
        def _():
            near(2, side).start()

    @pl.when(cut == 0)
    def _():
        first = restricted(s0[0, :, 8 : 8 + rows, :].reshape(2 * rows, cols), tbuf)
        for m in range(2):
            grid_c[0, m, crow : 2 * crow, :] = first[m * crow : (m + 1) * crow]
        each_coarse_send(0, lc, True, lambda copy: copy.start())

    for side in (0, 2):
        @on_side(side)
        def _():
            near(0, 2 - side).wait_recv()
    above = lookup(zt[...])
    below = lookup(zb[...])
    for m in range(2):
        rf[m, 0:8, :] = above[m]
        rf[m, rows + 8 : rows + 16, :] = below[m]

    def lateral(value, edge, col):
        width = value.shape[1]
        left = jnp.where(col == 0, edge, pltpu.roll(value, 1, 1))
        right = jnp.where(col == width - 1, edge, pltpu.roll(value, width - 1, 1))
        return 0.5 * (value + left), 0.5 * (value + right)

    def five(center, up, down, edge, col):
        west, east = lateral(center, edge, col)
        north = 0.5 * (center + up)
        south = 0.5 * (center + down)
        width = center.shape[1]
        return (
            jnp.where(col == width - 1, 0.0, east),
            jnp.where(col == 0, 0.0, west),
            north,
            south,
            (west + east) + (north + south),
        )

    for m in range(2):
        for i in range(chunks):
            low = 8 + 8 * i
            made = five(
                rf[m, low : low + 8, :], rf[m, low - 1 : low + 7, :],
                rf[m, low + 1 : low + 9, :], mat_ref[m, 0], col8,
            )
            for k in range(5):
                wt[m, k, 8 * i : 8 * i + 8, :] = made[k]

    def spread_sum(weights, center, up, down):
        width = center.shape[1]
        east, west, north, south, whole = weights
        total = east * pltpu.roll(center, width - 1, 1) + west * pltpu.roll(center, 1, 1)
        return (total + (north * up + south * down)) - whole * center

    def amps_at(slice_no, offset):
        return current_ref[bounds_ref[slice_no] + offset].astype(F32) * 0.001

    amps = [[amps_at(base + n, j) for j in range(2)] for n in range(lc)]

    def both(top, bottom):
        shape = (2 * half, cols)
        return jnp.where(rowh < half, jnp.broadcast_to(top, shape), jnp.broadcast_to(bottom, shape))

    edge_weights = []
    for m in range(2):
        center = both(rf[m, 7:8, :], rf[m, rows + 8 : rows + 9, :])
        outer = both(rf[m, 6:7, :], rf[m, rows + 9 : rows + 10, :])
        inner = both(rf[m, 8:9, :], rf[m, rows + 7 : rows + 8, :])
        edge_weights.append(five(center, outer, inner, mat_ref[m, 0], colh))
    edge_keep, edge_mix = link_factors(both(above[2][7:8], below[2][0:1]), 1.0)
    edge_amps = jnp.zeros((2 * half, cols), F32)
    for n in range(lc):
        edge_amps = jnp.where(
            jnp.logical_or(rowh == n, rowh == half + n), amps[n][0], edge_amps
        )
    edge_turn = both(above[3][7:8], below[3][0:1]) * edge_amps

    for side in (0, 2):
        @on_side(side)
        def _():
            near(1, 2 - side).wait_recv()

    edge_sums = []
    for m in range(2):
        center = jnp.where(rowh < half, ht[m], hb[m])
        outer = pltpu.roll(jnp.where(rowh < half, hb[m], ht[m]), half, 0)
        inner = pltpu.roll(jnp.where(rowh < half, md[m], mu[m]), half, 0)
        edge_sums.append((center, spread_sum(edge_weights[m], center, outer, inner)))
        for n in range(lc):
            s0[n, m, 7:8, :] = ht[m, n : n + 1, :]
            s0[n, m, rows + 8 : rows + 9, :] = hb[m, half + n : half + n + 1, :]
    edge_out = advance(edge_sums, edge_turn, edge_keep, edge_mix)
    inside = jnp.where(
        rowh < half, jnp.where(has_up, 1, 0), jnp.where(has_down, 1, 0)
    ) > 0
    for m in range(2):
        kept = jnp.where(inside, edge_out[m], 0.0)
        for n in range(lc):
            s1[n, m, 7:8, :] = kept[n : n + 1]
            s1[n, m, rows + 8 : rows + 9, :] = kept[half + n : half + n + 1]

    def fine_chunk(source, n, i, amperes):
        low = 8 + 8 * i
        at = slice(8 * i, 8 * i + 8)
        sums = []
        for m in range(2):
            center = source[n, m, low : low + 8, :]
            weights = [wt[m, k, at, :] for k in range(5)]
            sums.append((center, spread_sum(
                weights, center, source[n, m, low - 1 : low + 7, :],
                source[n, m, low + 1 : low + 9, :],
            )))
        return advance(sums, pqs[2, at, :] * amperes, pqs[0, at, :], pqs[1, at, :])

    for n in range(lc):
        for i in range(chunks):
            out = fine_chunk(s0, n, i, amps[n][0])
            for m in range(2):
                s1[n, m, 8 + 8 * i : 16 + 8 * i, :] = out[m]
        for i in range(chunks):
            out = fine_chunk(s1, n, i, amps[n][1])
            for m in range(2):
                ends_ref[n, m, 8 * i : 8 * i + 8, :] = out[m]
        mean = restricted(ends_ref[n].reshape(2 * rows, cols), tbuf)
        for m in range(2):
            grid_c[base + n + 1, m, crow : 2 * crow, :] = (
                mean[m * crow : (m + 1) * crow] - prev_ref[n, m]
            )
        each_coarse_send(base + n + 1, n, n < lc - 1, lambda copy: copy.start())

    for side in (0, 2):
        @on_side(side)
        def _():
            near(2, 2 - side).wait_recv()
    tall = 3 * crow
    crows = lax.broadcasted_iota(jnp.int32, (tall, ccol), 0)
    ccols = lax.broadcasted_iota(jnp.int32, (tall, ccol), 1)
    in_grid = jnp.logical_and(
        jnp.where(crows < crow, jnp.where(has_up, 1, 0), 1) > 0,
        jnp.where(crows >= 2 * crow, jnp.where(has_down, 1, 0), 1) > 0,
    )
    coarse_weights = []
    for m in range(2):
        center = cf[m] * 0.125
        coarse_weights.append(five(
            center, pltpu.roll(center, 1, 0), pltpu.roll(center, tall - 1, 0),
            mat_ref[m, 0] * 0.125, ccols,
        ))
    coarse_keep, coarse_mix = link_factors(cf[2], 2.0)
    coarse_turn = 2.0 * cf[3]

    def coarse_step(state, amperes):
        sums = []
        for m in range(2):
            center = state[m]
            sums.append((center, spread_sum(
                coarse_weights[m], center, pltpu.roll(center, 1, 0),
                pltpu.roll(center, tall - 1, 0),
            )))
        return advance(sums, coarse_turn * amperes, coarse_keep, coarse_mix)

    def following(out, g):
        return [jnp.where(in_grid, out[m] + grid_c[g, m], 0.0) for m in range(2)]

    @pl.when(cut > 0)
    def _():
        await_coarse(1, 0)
    for side in (0, 2):
        @on_side(side)
        def _():
            await_coarse(side, 0)
    for m in range(2):
        ybuf[m] = grid_c[0, m]
    for before in range(cuts - 1):
        @pl.when(cut > before)
        def _():
            state = [ybuf[m] for m in range(2)]
            for n in range(lc):
                slice_no = before * lc + n
                out = coarse_step(state, amps_at(slice_no, 0))
                await_coarse(1, slice_no + 1)
                for side in (0, 2):
                    @on_side(side)
                    def _():
                        await_coarse(side, slice_no + 1)
                state = following(out, slice_no + 1)
            for m in range(2):
                ybuf[m] = state[m]

    for n in range(lc - 1):
        for side in (0, 2):
            @on_side(side)
            def _():
                await_coarse(side, base + n + 1)
    state = [ybuf[m] for m in range(2)]
    for n in range(lc):
        out = coarse_step(state, amps[n][0])
        for m in range(2):
            fresh = out[m][crow : 2 * crow]
            new_ref[n, m] = fresh
            gain = fresh - prev_ref[n, m]
            for part in range(4):
                pbuf[n, pl.ds(m * rows + part, crow, stride=4), :] = gain
        if n < lc - 1:
            state = following(out, base + n + 1)
    for n in range(lc):
        added = jnp.dot(pieces(pbuf[n]), spread_ref[...], preferred_element_type=F32)
        ends_ref[n] = ends_ref[n] + added.reshape(2, rows, cols)

    for what in range(3):
        for side in (0, 2):
            @on_side(side)
            def _():
                near(what, side).wait_send()

    @pl.when(cut == 0)
    def _():
        each_coarse_send(0, lc, True, lambda copy: copy.wait_send())
    for n in range(lc):
        each_coarse_send(base + n + 1, n, n < lc - 1, lambda copy: copy.wait_send())


def solution(mesh):
    cuts, nsub = mesh.shape["cuts"], mesh.shape["sub"]
    tiles = mesh.shape["space"] * nsub

    def local(starts, coarse_prev, zone_ids, materials, current, bounds):
        lc, _, rows, cols = starts.shape
        crow, ccol = rows // 4, cols // 4
        half = max(4, lc)
        slices = lc * cuts
        sizes = (cuts, nsub, tiles, lc, rows, cols, materials.shape[1], half)
        match = lax.broadcasted_iota(jnp.int32, (ccol, cols), 1) // 4
        spread = (match == lax.broadcasted_iota(jnp.int32, (ccol, cols), 0)).astype(F32)
        gather = (spread.T * 0.0625).astype(BF16)
        gather = jnp.concatenate([gather, gather], axis=0)
        spread = spread.astype(BF16)
        spread = jnp.concatenate([spread, spread], axis=0)
        vmem = pl.BlockSpec(memory_space=pltpu.VMEM)
        smem = pl.BlockSpec(memory_space=pltpu.SMEM)
        return pl.pallas_call(
            functools.partial(kernel, sizes),
            out_shape=(
                jax.ShapeDtypeStruct(starts.shape, F32),
                jax.ShapeDtypeStruct(coarse_prev.shape, F32),
            ),
            in_specs=[pl.BlockSpec(memory_space=pl.ANY), vmem, vmem, smem, smem, smem, vmem, vmem],
            out_specs=(vmem, vmem),
            scratch_shapes=[
                pltpu.VMEM((lc, 2, rows + 16, cols), F32),
                pltpu.VMEM((lc, 2, rows + 16, cols), F32),
                pltpu.VMEM((2, rows + 16, cols), F32),
                pltpu.VMEM((4, rows, cols), F32),
                pltpu.VMEM((2, 5, rows, cols), F32),
                pltpu.VMEM((3, rows, cols), F32),
                pltpu.VMEM((8, cols), jnp.int32),
                pltpu.VMEM((8, cols), jnp.int32),
                pltpu.VMEM((2, 2 * half, cols), F32),
                pltpu.VMEM((2, 2 * half, cols), F32),
                pltpu.VMEM((2, 2 * half, cols), F32),
                pltpu.VMEM((2, 2 * half, cols), F32),
                pltpu.VMEM((4, 3 * crow, ccol), F32),
                pltpu.VMEM((slices + 1, 2, 3 * crow, ccol), F32),
                pltpu.VMEM((4 * rows, ccol), F32),
                pltpu.VMEM((lc, 2 * rows, ccol), F32),
                pltpu.VMEM((2, 3 * crow, ccol), F32),
                pltpu.SemaphoreType.DMA((1,)),
                pltpu.SemaphoreType.DMA((lc,)),
                pltpu.SemaphoreType.DMA((3, 2)),
                pltpu.SemaphoreType.DMA((3, 2)),
                pltpu.SemaphoreType.DMA((cuts, 3, lc + 1)),
                pltpu.SemaphoreType.DMA((3, slices + 1)),
            ],
            compiler_params=pltpu.CompilerParams(
                collective_id=0, has_side_effects=True, vmem_limit_bytes=32 * 1024 * 1024
            ),
        )(starts, coarse_prev, zone_ids, materials, current, bounds, gather, spread)

    placed = (
        P(("grp", "cuts"), None, ("space", "sub"), None),
        P(("grp", "cuts"), None, ("space", "sub"), None),
        P(("grp", "space", "sub"), None),
        P(),
        P("grp"),
        P(),
    )
    return jax.shard_map(
        local,
        mesh=mesh,
        in_specs=placed,
        out_specs=(
            P(("grp", "cuts"), None, ("space", "sub"), None),
            P(("grp", "cuts"), None, ("space", "sub"), None),
        ),
        check_vma=False,
    )
```

```python
import functools
import jax
import jax.numpy as jnp
from jax import lax
from jax.experimental import pallas as pl
from jax.experimental.pallas import tpu as pltpu
from jax.sharding import PartitionSpec as P

JOULE_GAIN = 0.5
MESH = pl.DeviceIdType.MESH
F32 = jnp.float32
BF16 = jnp.bfloat16


def pieces(values):
    high = values.astype(BF16)
    low = (values - high.astype(F32)).astype(BF16)
    return jnp.concatenate([high, low], axis=1)


def advance(sums, turn_amps, keep, mix):
    change = sums[0][1] + turn_amps
    magnet = sums[0][0] + change
    thermal = sums[1][0] + sums[1][1] + JOULE_GAIN * change * change
    return keep * magnet + mix * thermal, mix * magnet + keep * thermal


def link_factors(coupling, span):
    coupled = span * coupling
    diagonal = 1.0 + coupled
    offdiag = 0.5 * coupled
    determinant = diagonal * diagonal - offdiag * offdiag
    return diagonal / determinant, offdiag / determinant


def kernel(
    sizes, starts_hbm, prev_hbm, zone_hbm, mat_ref, current_ref, bounds_ref,
    ends_ref, new_ref, pbuf, spread_ref,
    prev_ref, zone_ref, gather_ref, s0, s1, rf, fl, wt, pqs, zt, zb, mu, md, ht, hb, cf, grid_c, tbuf, ybuf,
    in_sem, send_near, recv_near, send_c, recv_c,
):
    cuts, nsub, tiles, lc, rows, cols, zones, half = sizes
    crow, ccol = rows // 4, cols // 4
    chunks = rows // 8
    cut = lax.axis_index("cuts")
    tile = lax.axis_index("space") * nsub + lax.axis_index("sub")
    has_up = tile > 0
    has_down = tile < tiles - 1
    base = cut * lc

    def where_is(side, cut_no=None):
        other = tile + (side - 1)
        place = {"space": lax.div(other, nsub), "sub": lax.rem(other, nsub)}
        if cut_no is not None:
            place["cuts"] = cut_no
        return place

    def on_side(side):
        if side == 1:
            return lambda fn: fn()
        return pl.when(has_up if side == 0 else has_down)

    load_zone = pltpu.make_async_copy(zone_hbm, zone_ref, in_sem.at[1])
    load_zone.start()
    load = pltpu.make_async_copy(starts_hbm, s0.at[:, :, pl.ds(8, rows), :], in_sem.at[0])
    load.start()
    load_prev = pltpu.make_async_copy(prev_hbm, prev_ref, in_sem.at[2])
    load_prev.start()

    barrier = pltpu.get_barrier_semaphore()
    for side in (0, 2):
        @on_side(side)
        def _():
            pl.semaphore_signal(barrier, inc=1, device_id=where_is(side), device_id_type=MESH)
    for step in range(1, cuts):
        other_cut = lax.rem(cut + step, cuts)
        for side in range(3):
            @on_side(side)
            def _():
                pl.semaphore_signal(
                    barrier, inc=1, device_id=where_is(side, other_cut), device_id_type=MESH
                )

    row8 = lax.broadcasted_iota(jnp.int32, (8, cols), 0)
    col8 = lax.broadcasted_iota(jnp.int32, (8, cols), 1)
    rowh = lax.broadcasted_iota(jnp.int32, (2 * half, cols), 0)
    colh = lax.broadcasted_iota(jnp.int32, (2 * half, cols), 1)

    def lookup(zone):
        found = [jnp.full(zone.shape, mat_ref[m, 0], F32) for m in range(4)]
        for zone_no in range(1, zones):
            present = zone == zone_no
            found = [jnp.where(present, mat_ref[m, zone_no], found[m]) for m in range(4)]
        return found

    def restricted(values, buf):
        count = values.shape[0]
        buf[0:count, :] = jnp.dot(
            pieces(values), gather_ref[...], preferred_element_type=F32
        )
        total = buf[pl.ds(0, count // 4, stride=4), :]
        for part in range(1, 4):
            total = total + buf[pl.ds(part, count // 4, stride=4), :]
        return total

    tall_row = lax.broadcasted_iota(jnp.int32, (cols, ccol), 0)
    tall_col = lax.broadcasted_iota(jnp.int32, (cols, ccol), 1)
    wide_row = lax.broadcasted_iota(jnp.int32, (ccol, cols), 0)
    wide_col = lax.broadcasted_iota(jnp.int32, (ccol, cols), 1)
    gather = jnp.where((tall_row >> 2) == tall_col, 0.0625, 0.0).astype(BF16)
    spread = jnp.where((wide_col >> 2) == wide_row, 1.0, 0.0).astype(BF16)
    for part in range(2):
        gather_ref[part * cols : (part + 1) * cols, :] = gather
        spread_ref[part * ccol : (part + 1) * ccol, :] = spread

    load_zone.wait()
    for i in range(chunks):
        found = lookup(zone_ref[8 * i : 8 * i + 8, :])
        for m in range(4):
            fl[m, 8 * i : 8 * i + 8, :] = found[m]
        for m in range(2):
            rf[m, 8 + 8 * i : 16 + 8 * i, :] = found[m]
        keep, mix = link_factors(found[2], 1.0)
        pqs[0, 8 * i : 8 * i + 8, :] = keep
        pqs[1, 8 * i : 8 * i + 8, :] = mix
        pqs[2, 8 * i : 8 * i + 8, :] = found[3]

    load.wait()
    if lc < half:
        mu[...] = jnp.zeros(mu.shape, F32)
        md[...] = jnp.zeros(md.shape, F32)
    for n in range(lc):
        for m in range(2):
            mu[m, half + n : half + n + 1, :] = s0[n, m, 8:9, :]
            mu[m, n : n + 1, :] = s0[n, m, 9:10, :]
            md[m, n : n + 1, :] = s0[n, m, rows + 7 : rows + 8, :]
            md[m, half + n : half + n + 1, :] = s0[n, m, rows + 6 : rows + 7, :]

    ups = jnp.where(has_up, 1, 0) + jnp.where(has_down, 1, 0)
    pl.semaphore_wait(barrier, ups + (cuts - 1) * (1 + ups))

    def near(what, side):
        if what == 0:
            source = zone_ref.at[0:8] if side == 0 else zone_ref.at[rows - 8 : rows]
            target = zb if side == 0 else zt
        elif what == 1:
            source = mu if side == 0 else md
            target = hb if side == 0 else ht
        else:
            source = cf.at[:, pl.ds(crow, crow), :]
            target = cf.at[:, pl.ds(2 * crow if side == 0 else 0, crow), :]
        return pltpu.make_async_remote_copy(
            src_ref=source,
            dst_ref=target,
            send_sem=send_near.at[what, side // 2],
            recv_sem=recv_near.at[what, side // 2],
            device_id=where_is(side),
            device_id_type=MESH,
        )

    def coarse_copy(side, g, local_no, dest):
        return pltpu.make_async_remote_copy(
            src_ref=grid_c.at[g, :, pl.ds(crow, crow), :],
            dst_ref=grid_c.at[g, :, pl.ds((2 - side) * crow, crow), :],
            send_sem=send_c.at[dest, side, local_no],
            recv_sem=recv_c.at[2 - side, g],
            device_id=where_is(side, None if dest == 0 else dest),
            device_id_type=MESH,
        )

    def each_coarse_send(g, local_no, nearby, action):
        for dest in range(1, cuts):
            @pl.when(cut < dest)
            def _():
                for side in (1, 0, 2):
                    @on_side(side)
                    def _():
                        action(coarse_copy(side, g, local_no, dest))
        if nearby:
            for side in (0, 2):
                @on_side(side)
                def _():
                    action(coarse_copy(side, g, local_no, 0))

    def await_coarse(side, g):
        pltpu.make_async_remote_copy(
            src_ref=grid_c.at[g, :, pl.ds(crow, crow), :],
            dst_ref=grid_c.at[g, :, pl.ds(side * crow, crow), :],
            send_sem=send_c.at[0, 0, 0],
            recv_sem=recv_c.at[side, g],
            device_id=where_is(1, lax.rem(cut + 1, cuts)),
            device_id_type=MESH,
        ).wait_recv()

    for what in (0, 1):
        for side in (0, 2):
            @on_side(side)
            def _():
                near(what, side).start()

    @pl.when(jnp.logical_not(has_up))
    def _():
        zt[...] = jnp.zeros(zt.shape, jnp.int32)
        ht[...] = jnp.zeros(ht.shape, F32)
        for m in range(4):
            cf[m, 0:crow, :] = jnp.full((crow, ccol), mat_ref[m, 0], F32)
        grid_c[:, :, 0:crow, :] = jnp.zeros(grid_c.shape[:2] + (crow, ccol), F32)

    @pl.when(jnp.logical_not(has_down))
    def _():
        zb[...] = jnp.zeros(zb.shape, jnp.int32)
        hb[...] = jnp.zeros(hb.shape, F32)
        for m in range(4):
            cf[m, 2 * crow : 3 * crow, :] = jnp.full((crow, ccol), mat_ref[m, 0], F32)
        grid_c[:, :, 2 * crow : 3 * crow, :] = jnp.zeros(grid_c.shape[:2] + (crow, ccol), F32)

    own_c = restricted(fl[...].reshape(4 * rows, cols), tbuf)
    for m in range(4):
        cf[m, crow : 2 * crow, :] = own_c[m * crow : (m + 1) * crow]
    for side in (0, 2):
        @on_side(side)
        def _():
            near(2, side).start()

    @pl.when(cut == 0)
    def _():
        first = restricted(s0[0, :, 8 : 8 + rows, :].reshape(2 * rows, cols), tbuf)
        for m in range(2):
            grid_c[0, m, crow : 2 * crow, :] = first[m * crow : (m + 1) * crow]
        each_coarse_send(0, lc, True, lambda copy: copy.start())

    def lateral(value, edge, col):
        width = value.shape[1]
        left = jnp.where(col == 0, edge, pltpu.roll(value, 1, 1))
        right = jnp.where(col == width - 1, edge, pltpu.roll(value, width - 1, 1))
        return 0.5 * (value + left), 0.5 * (value + right)

    def five(center, up, down, edge, col):
        west, east = lateral(center, edge, col)
        north = 0.5 * (center + up)
        south = 0.5 * (center + down)
        width = center.shape[1]
        return (
            jnp.where(col == width - 1, 0.0, east),
            jnp.where(col == 0, 0.0, west),
            north,
            south,
            (west + east) + (north + south),
        )

    def make_weights(i):
        low = 8 + 8 * i
        for m in range(2):
            made = five(
                rf[m, low : low + 8, :], rf[m, low - 1 : low + 7, :],
                rf[m, low + 1 : low + 9, :], mat_ref[m, 0], col8,
            )
            for k in range(5):
                wt[m, k, 8 * i : 8 * i + 8, :] = made[k]

    def spread_sum(weights, center, up, down):
        width = center.shape[1]
        east, west, north, south, whole = weights
        total = east * pltpu.roll(center, width - 1, 1) + west * pltpu.roll(center, 1, 1)
        return (total + (north * up + south * down)) - whole * center

    def amps_at(slice_no, offset):
        return current_ref[bounds_ref[slice_no] + offset].astype(F32) * 0.001

    amps = [[amps_at(base + n, j) for j in range(2)] for n in range(lc)]

    def fine_chunk(source, n, i, amperes):
        low = 8 + 8 * i
        at = slice(8 * i, 8 * i + 8)
        sums = []
        for m in range(2):
            center = source[n, m, low : low + 8, :]
            weights = [wt[m, k, at, :] for k in range(5)]
            sums.append((center, spread_sum(
                weights, center, source[n, m, low - 1 : low + 7, :],
                source[n, m, low + 1 : low + 9, :],
            )))
        return advance(sums, pqs[2, at, :] * amperes, pqs[0, at, :], pqs[1, at, :])

    def first_step(n, i):
        out = fine_chunk(s0, n, i, amps[n][0])
        for m in range(2):
            s1[n, m, 8 + 8 * i : 16 + 8 * i, :] = out[m]

    for i in range(1, chunks - 1):
        make_weights(i)
    for n in range(lc):
        for i in range(1, chunks - 1):
            first_step(n, i)

    for side in (0, 2):
        @on_side(side)
        def _():
            near(0, 2 - side).wait_recv()
    above = lookup(zt[...])
    below = lookup(zb[...])
    for m in range(2):
        rf[m, 0:8, :] = above[m]
        rf[m, rows + 8 : rows + 16, :] = below[m]

    for i in (0, chunks - 1):
        make_weights(i)

    def both(top, bottom):
        shape = (2 * half, cols)
        return jnp.where(rowh < half, jnp.broadcast_to(top, shape), jnp.broadcast_to(bottom, shape))

    edge_weights = []
    for m in range(2):
        center = both(rf[m, 7:8, :], rf[m, rows + 8 : rows + 9, :])
        outer = both(rf[m, 6:7, :], rf[m, rows + 9 : rows + 10, :])
        inner = both(rf[m, 8:9, :], rf[m, rows + 7 : rows + 8, :])
        edge_weights.append(five(center, outer, inner, mat_ref[m, 0], colh))
    edge_keep, edge_mix = link_factors(both(above[2][7:8], below[2][0:1]), 1.0)
    edge_amps = jnp.zeros((2 * half, cols), F32)
    for n in range(lc):
        edge_amps = jnp.where(
            jnp.logical_or(rowh == n, rowh == half + n), amps[n][0], edge_amps
        )
    edge_turn = both(above[3][7:8], below[3][0:1]) * edge_amps

    for side in (0, 2):
        @on_side(side)
        def _():
            near(1, 2 - side).wait_recv()

    edge_sums = []
    for m in range(2):
        center = jnp.where(rowh < half, ht[m], hb[m])
        outer = pltpu.roll(jnp.where(rowh < half, hb[m], ht[m]), half, 0)
        inner = pltpu.roll(jnp.where(rowh < half, md[m], mu[m]), half, 0)
        edge_sums.append((center, spread_sum(edge_weights[m], center, outer, inner)))
        for n in range(lc):
            s0[n, m, 7:8, :] = ht[m, n : n + 1, :]
            s0[n, m, rows + 8 : rows + 9, :] = hb[m, half + n : half + n + 1, :]
    edge_out = advance(edge_sums, edge_turn, edge_keep, edge_mix)
    inside = jnp.where(
        rowh < half, jnp.where(has_up, 1, 0), jnp.where(has_down, 1, 0)
    ) > 0
    for m in range(2):
        kept = jnp.where(inside, edge_out[m], 0.0)
        for n in range(lc):
            s1[n, m, 7:8, :] = kept[n : n + 1]
            s1[n, m, rows + 8 : rows + 9, :] = kept[half + n : half + n + 1]

    load_prev.wait()
    for n in range(lc):
        for i in (0, chunks - 1):
            first_step(n, i)
        for i in range(chunks):
            out = fine_chunk(s1, n, i, amps[n][1])
            for m in range(2):
                ends_ref[n, m, 8 * i : 8 * i + 8, :] = out[m]
        mean = restricted(ends_ref[n].reshape(2 * rows, cols), tbuf)
        for m in range(2):
            grid_c[base + n + 1, m, crow : 2 * crow, :] = (
                mean[m * crow : (m + 1) * crow] - prev_ref[n, m]
            )
        each_coarse_send(base + n + 1, n, n < lc - 1, lambda copy: copy.start())

    for side in (0, 2):
        @on_side(side)
        def _():
            near(2, 2 - side).wait_recv()
    tall = 3 * crow
    crows = lax.broadcasted_iota(jnp.int32, (tall, ccol), 0)
    ccols = lax.broadcasted_iota(jnp.int32, (tall, ccol), 1)
    in_grid = jnp.logical_and(
        jnp.where(crows < crow, jnp.where(has_up, 1, 0), 1) > 0,
        jnp.where(crows >= 2 * crow, jnp.where(has_down, 1, 0), 1) > 0,
    )
    coarse_weights = []
    for m in range(2):
        center = cf[m] * 0.125
        coarse_weights.append(five(
            center, pltpu.roll(center, 1, 0), pltpu.roll(center, tall - 1, 0),
            mat_ref[m, 0] * 0.125, ccols,
        ))
    coarse_keep, coarse_mix = link_factors(cf[2], 2.0)
    coarse_turn = 2.0 * cf[3]

    def coarse_step(state, amperes):
        sums = []
        for m in range(2):
            center = state[m]
            sums.append((center, spread_sum(
                coarse_weights[m], center, pltpu.roll(center, 1, 0),
                pltpu.roll(center, tall - 1, 0),
            )))
        return advance(sums, coarse_turn * amperes, coarse_keep, coarse_mix)

    def following(out, g):
        return [jnp.where(in_grid, out[m] + grid_c[g, m], 0.0) for m in range(2)]

    @pl.when(cut > 0)
    def _():
        await_coarse(1, 0)
    for side in (0, 2):
        @on_side(side)
        def _():
            await_coarse(side, 0)
    for m in range(2):
        ybuf[m] = grid_c[0, m]
    for before in range(cuts - 1):
        @pl.when(cut > before)
        def _():
            state = [ybuf[m] for m in range(2)]
            for n in range(lc):
                slice_no = before * lc + n
                out = coarse_step(state, amps_at(slice_no, 0))
                await_coarse(1, slice_no + 1)
                for side in (0, 2):
                    @on_side(side)
                    def _():
                        await_coarse(side, slice_no + 1)
                state = following(out, slice_no + 1)
            for m in range(2):
                ybuf[m] = state[m]

    for n in range(lc - 1):
        for side in (0, 2):
            @on_side(side)
            def _():
                await_coarse(side, base + n + 1)
    state = [ybuf[m] for m in range(2)]
    for n in range(lc):
        out = coarse_step(state, amps[n][0])
        for m in range(2):
            fresh = out[m][crow : 2 * crow]
            new_ref[n, m] = fresh
            gain = fresh - prev_ref[n, m]
            for part in range(4):
                pbuf[n, pl.ds(m * rows + part, crow, stride=4), :] = gain
        if n < lc - 1:
            state = following(out, base + n + 1)

    for what in range(3):
        for side in (0, 2):
            @on_side(side)
            def _():
                near(what, side).wait_send()

    @pl.when(cut == 0)
    def _():
        each_coarse_send(0, lc, True, lambda copy: copy.wait_send())
    for n in range(lc):
        each_coarse_send(base + n + 1, n, n < lc - 1, lambda copy: copy.wait_send())


def finish(fine_ref, new_ref, pbuf, spread_ref, ends_out, new_out, total, sems):
    lc, _, rows, cols = fine_ref.shape
    copies = [pltpu.make_async_copy(new_ref, new_out, sems.at[lc])]
    copies[0].start()
    for n in range(lc):
        added = jnp.dot(pieces(pbuf[n]), spread_ref[...], preferred_element_type=F32)
        total[n] = fine_ref[n] + added.reshape(2, rows, cols)
        copies.append(pltpu.make_async_copy(total.at[n], ends_out.at[n], sems.at[n]))
        copies[-1].start()
    for copy in copies:
        copy.wait()


def solution(mesh):
    cuts, nsub = mesh.shape["cuts"], mesh.shape["sub"]
    tiles = mesh.shape["space"] * nsub

    def local(starts, coarse_prev, zone_ids, materials, current, bounds):
        lc, _, rows, cols = starts.shape
        crow, ccol = rows // 4, cols // 4
        half = max(4, lc)
        slices = lc * cuts
        sizes = (cuts, nsub, tiles, lc, rows, cols, materials.shape[1], half)
        vmem = pl.BlockSpec(memory_space=pltpu.VMEM)
        smem = pl.BlockSpec(memory_space=pltpu.SMEM)
        hbm = pl.BlockSpec(memory_space=pltpu.HBM)
        fine, new, risen, spread = pl.pallas_call(
            functools.partial(kernel, sizes),
            out_shape=(
                jax.ShapeDtypeStruct(starts.shape, F32),
                jax.ShapeDtypeStruct(coarse_prev.shape, F32),
                jax.ShapeDtypeStruct((lc, 2 * rows, ccol), F32),
                jax.ShapeDtypeStruct((2 * ccol, cols), BF16),
            ),
            in_specs=[hbm, hbm, hbm, smem, smem, smem],
            out_specs=(vmem,) * 4,
            scratch_shapes=[
                pltpu.VMEM((lc, 2, crow, ccol), F32),
                pltpu.VMEM((rows, cols), jnp.int32),
                pltpu.VMEM((2 * cols, ccol), BF16),
                pltpu.VMEM((lc, 2, rows + 16, cols), F32),
                pltpu.VMEM((lc, 2, rows + 16, cols), F32),
                pltpu.VMEM((2, rows + 16, cols), F32),
                pltpu.VMEM((4, rows, cols), F32),
                pltpu.VMEM((2, 5, rows, cols), F32),
                pltpu.VMEM((3, rows, cols), F32),
                pltpu.VMEM((8, cols), jnp.int32),
                pltpu.VMEM((8, cols), jnp.int32),
                pltpu.VMEM((2, 2 * half, cols), F32),
                pltpu.VMEM((2, 2 * half, cols), F32),
                pltpu.VMEM((2, 2 * half, cols), F32),
                pltpu.VMEM((2, 2 * half, cols), F32),
                pltpu.VMEM((4, 3 * crow, ccol), F32),
                pltpu.VMEM((slices + 1, 2, 3 * crow, ccol), F32),
                pltpu.VMEM((4 * rows, ccol), F32),
                pltpu.VMEM((2, 3 * crow, ccol), F32),
                pltpu.SemaphoreType.DMA((3,)),
                pltpu.SemaphoreType.DMA((3, 2)),
                pltpu.SemaphoreType.DMA((3, 2)),
                pltpu.SemaphoreType.DMA((cuts, 3, lc + 1)),
                pltpu.SemaphoreType.DMA((3, slices + 1)),
            ],
            compiler_params=pltpu.CompilerParams(
                collective_id=0, has_side_effects=True, vmem_limit_bytes=32 * 1024 * 1024
            ),
        )(starts, coarse_prev, zone_ids, materials, current, bounds)
        return pl.pallas_call(
            finish,
            out_shape=(
                jax.ShapeDtypeStruct(starts.shape, F32),
                jax.ShapeDtypeStruct(coarse_prev.shape, F32),
            ),
            in_specs=[vmem] * 4,
            out_specs=(hbm, hbm),
            scratch_shapes=[
                pltpu.VMEM(starts.shape, F32),
                pltpu.SemaphoreType.DMA((lc + 1,)),
            ],
            compiler_params=pltpu.CompilerParams(vmem_limit_bytes=16 * 1024 * 1024),
        )(fine, new, risen, spread)

    placed = (
        P(("grp", "cuts"), None, ("space", "sub"), None),
        P(("grp", "cuts"), None, ("space", "sub"), None),
        P(("grp", "space", "sub"), None),
        P(),
        P("grp"),
        P(),
    )
    return jax.shard_map(
        local,
        mesh=mesh,
        in_specs=placed,
        out_specs=(
            P(("grp", "cuts"), None, ("space", "sub"), None),
            P(("grp", "cuts"), None, ("space", "sub"), None),
        ),
        check_vma=False,
    )
```

```python
import functools
import jax
import jax.numpy as jnp
from jax import lax
from jax.experimental import pallas as pl
from jax.experimental.pallas import tpu as pltpu
from jax.sharding import PartitionSpec as P

JOULE_GAIN = 0.5
MESH = pl.DeviceIdType.MESH
F32 = jnp.float32
BF16 = jnp.bfloat16


def pieces(values):
    high = values.astype(BF16)
    low = (values - high.astype(F32)).astype(BF16)
    return jnp.concatenate([high, low], axis=1)


def advance(sums, turn_amps, keep, mix):
    change = sums[0][1] + turn_amps
    magnet = sums[0][0] + change
    thermal = sums[1][0] + sums[1][1] + JOULE_GAIN * change * change
    return keep * magnet + mix * thermal, mix * magnet + keep * thermal


def link_factors(coupling, span):
    coupled = span * coupling
    diagonal = 1.0 + coupled
    offdiag = 0.5 * coupled
    determinant = diagonal * diagonal - offdiag * offdiag
    return diagonal / determinant, offdiag / determinant


def kernel(
    sizes, starts_hbm, prev_hbm, zone_hbm, mat_hbm, current_hbm, bounds_hbm,
    ends_ref, new_ref, pbuf, spread_ref,
    mat_ref, current_ref, bounds_ref, prev_ref, zone_ref, gather_ref, s0, s1, rf, fl, wt, pqs, zt, zb, mu, md, ht, hb, cf, grid_c, tbuf, ybuf,
    in_sem, send_near, recv_near, send_c, recv_c,
):
    cuts, nsub, tiles, lc, rows, cols, zones, half = sizes
    crow, ccol = rows // 4, cols // 4
    chunks = rows // 8
    cut = lax.axis_index("cuts")
    tile = lax.axis_index("space") * nsub + lax.axis_index("sub")
    has_up = tile > 0
    has_down = tile < tiles - 1
    base = cut * lc

    def where_is(side, cut_no=None):
        other = tile + (side - 1)
        place = {"space": lax.div(other, nsub), "sub": lax.rem(other, nsub)}
        if cut_no is not None:
            place["cuts"] = cut_no
        return place

    def on_side(side):
        if side == 1:
            return lambda fn: fn()
        return pl.when(has_up if side == 0 else has_down)

    load_zone = pltpu.make_async_copy(zone_hbm, zone_ref, in_sem.at[1])
    load_zone.start()
    small = [
        pltpu.make_async_copy(source, target, in_sem.at[3 + k])
        for k, (source, target) in enumerate(
            ((mat_hbm, mat_ref), (current_hbm, current_ref), (bounds_hbm, bounds_ref))
        )
    ]
    for copy in small:
        copy.start()
    load = pltpu.make_async_copy(starts_hbm, s0.at[:, :, pl.ds(8, rows), :], in_sem.at[0])
    load.start()
    load_prev = pltpu.make_async_copy(prev_hbm, prev_ref, in_sem.at[2])
    load_prev.start()

    barrier = pltpu.get_barrier_semaphore()
    for side in (0, 2):
        @on_side(side)
        def _():
            pl.semaphore_signal(barrier, inc=1, device_id=where_is(side), device_id_type=MESH)
    for step in range(1, cuts):
        other_cut = lax.rem(cut + step, cuts)
        for side in range(3):
            @on_side(side)
            def _():
                pl.semaphore_signal(
                    barrier, inc=1, device_id=where_is(side, other_cut), device_id_type=MESH
                )

    row8 = lax.broadcasted_iota(jnp.int32, (8, cols), 0)
    col8 = lax.broadcasted_iota(jnp.int32, (8, cols), 1)
    rowh = lax.broadcasted_iota(jnp.int32, (2 * half, cols), 0)
    colh = lax.broadcasted_iota(jnp.int32, (2 * half, cols), 1)

    def lookup(zone):
        found = [jnp.full(zone.shape, mat_ref[m, 0], F32) for m in range(4)]
        for zone_no in range(1, zones):
            present = zone == zone_no
            found = [jnp.where(present, mat_ref[m, zone_no], found[m]) for m in range(4)]
        return found

    def restricted(values, buf):
        count = values.shape[0]
        buf[0:count, :] = jnp.dot(
            pieces(values), gather_ref[...], preferred_element_type=F32
        )
        total = buf[pl.ds(0, count // 4, stride=4), :]
        for part in range(1, 4):
            total = total + buf[pl.ds(part, count // 4, stride=4), :]
        return total

    tall_row = lax.broadcasted_iota(jnp.int32, (cols, ccol), 0)
    tall_col = lax.broadcasted_iota(jnp.int32, (cols, ccol), 1)
    wide_row = lax.broadcasted_iota(jnp.int32, (ccol, cols), 0)
    wide_col = lax.broadcasted_iota(jnp.int32, (ccol, cols), 1)
    gather = jnp.where((tall_row >> 2) == tall_col, 0.0625, 0.0).astype(BF16)
    spread = jnp.where((wide_col >> 2) == wide_row, 1.0, 0.0).astype(BF16)
    for part in range(2):
        gather_ref[part * cols : (part + 1) * cols, :] = gather
        spread_ref[part * ccol : (part + 1) * ccol, :] = spread

    for copy in small:
        copy.wait()
    load_zone.wait()
    for i in range(chunks):
        found = lookup(zone_ref[8 * i : 8 * i + 8, :])
        for m in range(4):
            fl[m, 8 * i : 8 * i + 8, :] = found[m]
        for m in range(2):
            rf[m, 8 + 8 * i : 16 + 8 * i, :] = found[m]
        keep, mix = link_factors(found[2], 1.0)
        pqs[0, 8 * i : 8 * i + 8, :] = keep
        pqs[1, 8 * i : 8 * i + 8, :] = mix
        pqs[2, 8 * i : 8 * i + 8, :] = found[3]

    load.wait()
    if lc < half:
        mu[...] = jnp.zeros(mu.shape, F32)
        md[...] = jnp.zeros(md.shape, F32)
    for n in range(lc):
        for m in range(2):
            mu[m, half + n : half + n + 1, :] = s0[n, m, 8:9, :]
            mu[m, n : n + 1, :] = s0[n, m, 9:10, :]
            md[m, n : n + 1, :] = s0[n, m, rows + 7 : rows + 8, :]
            md[m, half + n : half + n + 1, :] = s0[n, m, rows + 6 : rows + 7, :]

    ups = jnp.where(has_up, 1, 0) + jnp.where(has_down, 1, 0)
    pl.semaphore_wait(barrier, ups + (cuts - 1) * (1 + ups))

    def near(what, side):
        if what == 0:
            source = zone_ref.at[0:8] if side == 0 else zone_ref.at[rows - 8 : rows]
            target = zb if side == 0 else zt
        elif what == 1:
            source = mu if side == 0 else md
            target = hb if side == 0 else ht
        else:
            source = cf.at[:, pl.ds(crow, crow), :]
            target = cf.at[:, pl.ds(2 * crow if side == 0 else 0, crow), :]
        return pltpu.make_async_remote_copy(
            src_ref=source,
            dst_ref=target,
            send_sem=send_near.at[what, side // 2],
            recv_sem=recv_near.at[what, side // 2],
            device_id=where_is(side),
            device_id_type=MESH,
        )

    def coarse_copy(side, g, local_no, dest):
        return pltpu.make_async_remote_copy(
            src_ref=grid_c.at[g, :, pl.ds(crow, crow), :],
            dst_ref=grid_c.at[g, :, pl.ds((2 - side) * crow, crow), :],
            send_sem=send_c.at[dest, side, local_no],
            recv_sem=recv_c.at[2 - side, g],
            device_id=where_is(side, None if dest == 0 else dest),
            device_id_type=MESH,
        )

    def each_coarse_send(g, local_no, nearby, action):
        for dest in range(1, cuts):
            @pl.when(cut < dest)
            def _():
                for side in (1, 0, 2):
                    @on_side(side)
                    def _():
                        action(coarse_copy(side, g, local_no, dest))
        if nearby:
            for side in (0, 2):
                @on_side(side)
                def _():
                    action(coarse_copy(side, g, local_no, 0))

    def await_coarse(side, g):
        pltpu.make_async_remote_copy(
            src_ref=grid_c.at[g, :, pl.ds(crow, crow), :],
            dst_ref=grid_c.at[g, :, pl.ds(side * crow, crow), :],
            send_sem=send_c.at[0, 0, 0],
            recv_sem=recv_c.at[side, g],
            device_id=where_is(1, lax.rem(cut + 1, cuts)),
            device_id_type=MESH,
        ).wait_recv()

    for what in (0, 1):
        for side in (0, 2):
            @on_side(side)
            def _():
                near(what, side).start()

    @pl.when(jnp.logical_not(has_up))
    def _():
        zt[...] = jnp.zeros(zt.shape, jnp.int32)
        ht[...] = jnp.zeros(ht.shape, F32)
        for m in range(4):
            cf[m, 0:crow, :] = jnp.full((crow, ccol), mat_ref[m, 0], F32)
        grid_c[:, :, 0:crow, :] = jnp.zeros(grid_c.shape[:2] + (crow, ccol), F32)

    @pl.when(jnp.logical_not(has_down))
    def _():
        zb[...] = jnp.zeros(zb.shape, jnp.int32)
        hb[...] = jnp.zeros(hb.shape, F32)
        for m in range(4):
            cf[m, 2 * crow : 3 * crow, :] = jnp.full((crow, ccol), mat_ref[m, 0], F32)
        grid_c[:, :, 2 * crow : 3 * crow, :] = jnp.zeros(grid_c.shape[:2] + (crow, ccol), F32)

    own_c = restricted(fl[...].reshape(4 * rows, cols), tbuf)
    for m in range(4):
        cf[m, crow : 2 * crow, :] = own_c[m * crow : (m + 1) * crow]
    for side in (0, 2):
        @on_side(side)
        def _():
            near(2, side).start()

    @pl.when(cut == 0)
    def _():
        first = restricted(s0[0, :, 8 : 8 + rows, :].reshape(2 * rows, cols), tbuf)
        for m in range(2):
            grid_c[0, m, crow : 2 * crow, :] = first[m * crow : (m + 1) * crow]
        each_coarse_send(0, lc, True, lambda copy: copy.start())

    def lateral(value, edge, col):
        width = value.shape[1]
        left = jnp.where(col == 0, edge, pltpu.roll(value, 1, 1))
        right = jnp.where(col == width - 1, edge, pltpu.roll(value, width - 1, 1))
        return 0.5 * (value + left), 0.5 * (value + right)

    def five(center, up, down, edge, col):
        west, east = lateral(center, edge, col)
        north = 0.5 * (center + up)
        south = 0.5 * (center + down)
        width = center.shape[1]
        return (
            jnp.where(col == width - 1, 0.0, east),
            jnp.where(col == 0, 0.0, west),
            north,
            south,
            (west + east) + (north + south),
        )

    def make_weights(i):
        low = 8 + 8 * i
        for m in range(2):
            made = five(
                rf[m, low : low + 8, :], rf[m, low - 1 : low + 7, :],
                rf[m, low + 1 : low + 9, :], mat_ref[m, 0], col8,
            )
            for k in range(5):
                wt[m, k, 8 * i : 8 * i + 8, :] = made[k]

    def spread_sum(weights, center, up, down):
        width = center.shape[1]
        east, west, north, south, whole = weights
        total = east * pltpu.roll(center, width - 1, 1) + west * pltpu.roll(center, 1, 1)
        return (total + (north * up + south * down)) - whole * center

    def amps_at(slice_no, offset):
        return current_ref[bounds_ref[slice_no] + offset].astype(F32) * 0.001

    amps = [[amps_at(base + n, j) for j in range(2)] for n in range(lc)]

    def fine_chunk(source, n, i, amperes):
        low = 8 + 8 * i
        at = slice(8 * i, 8 * i + 8)
        sums = []
        for m in range(2):
            center = source[n, m, low : low + 8, :]
            weights = [wt[m, k, at, :] for k in range(5)]
            sums.append((center, spread_sum(
                weights, center, source[n, m, low - 1 : low + 7, :],
                source[n, m, low + 1 : low + 9, :],
            )))
        return advance(sums, pqs[2, at, :] * amperes, pqs[0, at, :], pqs[1, at, :])

    def first_step(n, i):
        out = fine_chunk(s0, n, i, amps[n][0])
        for m in range(2):
            s1[n, m, 8 + 8 * i : 16 + 8 * i, :] = out[m]

    for i in range(1, chunks - 1):
        make_weights(i)
    for n in range(lc):
        for i in range(1, chunks - 1):
            first_step(n, i)

    for side in (0, 2):
        @on_side(side)
        def _():
            near(0, 2 - side).wait_recv()
    above = lookup(zt[...])
    below = lookup(zb[...])
    for m in range(2):
        rf[m, 0:8, :] = above[m]
        rf[m, rows + 8 : rows + 16, :] = below[m]

    for i in (0, chunks - 1):
        make_weights(i)

    def both(top, bottom):
        shape = (2 * half, cols)
        return jnp.where(rowh < half, jnp.broadcast_to(top, shape), jnp.broadcast_to(bottom, shape))

    edge_weights = []
    for m in range(2):
        center = both(rf[m, 7:8, :], rf[m, rows + 8 : rows + 9, :])
        outer = both(rf[m, 6:7, :], rf[m, rows + 9 : rows + 10, :])
        inner = both(rf[m, 8:9, :], rf[m, rows + 7 : rows + 8, :])
        edge_weights.append(five(center, outer, inner, mat_ref[m, 0], colh))
    edge_keep, edge_mix = link_factors(both(above[2][7:8], below[2][0:1]), 1.0)
    edge_amps = jnp.zeros((2 * half, cols), F32)
    for n in range(lc):
        edge_amps = jnp.where(
            jnp.logical_or(rowh == n, rowh == half + n), amps[n][0], edge_amps
        )
    edge_turn = both(above[3][7:8], below[3][0:1]) * edge_amps

    for side in (0, 2):
        @on_side(side)
        def _():
            near(1, 2 - side).wait_recv()

    edge_sums = []
    for m in range(2):
        center = jnp.where(rowh < half, ht[m], hb[m])
        outer = pltpu.roll(jnp.where(rowh < half, hb[m], ht[m]), half, 0)
        inner = pltpu.roll(jnp.where(rowh < half, md[m], mu[m]), half, 0)
        edge_sums.append((center, spread_sum(edge_weights[m], center, outer, inner)))
        for n in range(lc):
            s0[n, m, 7:8, :] = ht[m, n : n + 1, :]
            s0[n, m, rows + 8 : rows + 9, :] = hb[m, half + n : half + n + 1, :]
    edge_out = advance(edge_sums, edge_turn, edge_keep, edge_mix)
    inside = jnp.where(
        rowh < half, jnp.where(has_up, 1, 0), jnp.where(has_down, 1, 0)
    ) > 0
    for m in range(2):
        kept = jnp.where(inside, edge_out[m], 0.0)
        for n in range(lc):
            s1[n, m, 7:8, :] = kept[n : n + 1]
            s1[n, m, rows + 8 : rows + 9, :] = kept[half + n : half + n + 1]

    load_prev.wait()
    for n in range(lc):
        for i in (0, chunks - 1):
            first_step(n, i)
        for i in range(chunks):
            out = fine_chunk(s1, n, i, amps[n][1])
            for m in range(2):
                ends_ref[n, m, 8 * i : 8 * i + 8, :] = out[m]
        mean = restricted(ends_ref[n].reshape(2 * rows, cols), tbuf)
        for m in range(2):
            grid_c[base + n + 1, m, crow : 2 * crow, :] = (
                mean[m * crow : (m + 1) * crow] - prev_ref[n, m]
            )
        each_coarse_send(base + n + 1, n, n < lc - 1, lambda copy: copy.start())

    for side in (0, 2):
        @on_side(side)
        def _():
            near(2, 2 - side).wait_recv()
    tall = 3 * crow
    crows = lax.broadcasted_iota(jnp.int32, (tall, ccol), 0)
    ccols = lax.broadcasted_iota(jnp.int32, (tall, ccol), 1)
    in_grid = jnp.logical_and(
        jnp.where(crows < crow, jnp.where(has_up, 1, 0), 1) > 0,
        jnp.where(crows >= 2 * crow, jnp.where(has_down, 1, 0), 1) > 0,
    )
    coarse_weights = []
    for m in range(2):
        center = cf[m] * 0.125
        coarse_weights.append(five(
            center, pltpu.roll(center, 1, 0), pltpu.roll(center, tall - 1, 0),
            mat_ref[m, 0] * 0.125, ccols,
        ))
    coarse_keep, coarse_mix = link_factors(cf[2], 2.0)
    coarse_turn = 2.0 * cf[3]

    def coarse_step(state, amperes):
        sums = []
        for m in range(2):
            center = state[m]
            sums.append((center, spread_sum(
                coarse_weights[m], center, pltpu.roll(center, 1, 0),
                pltpu.roll(center, tall - 1, 0),
            )))
        return advance(sums, coarse_turn * amperes, coarse_keep, coarse_mix)

    def following(out, g):
        return [jnp.where(in_grid, out[m] + grid_c[g, m], 0.0) for m in range(2)]

    @pl.when(cut > 0)
    def _():
        await_coarse(1, 0)
    for side in (0, 2):
        @on_side(side)
        def _():
            await_coarse(side, 0)
    for m in range(2):
        ybuf[m] = grid_c[0, m]
    for before in range(cuts - 1):
        @pl.when(cut > before)
        def _():
            state = [ybuf[m] for m in range(2)]
            for n in range(lc):
                slice_no = before * lc + n
                out = coarse_step(state, amps_at(slice_no, 0))
                await_coarse(1, slice_no + 1)
                for side in (0, 2):
                    @on_side(side)
                    def _():
                        await_coarse(side, slice_no + 1)
                state = following(out, slice_no + 1)
            for m in range(2):
                ybuf[m] = state[m]

    for n in range(lc - 1):
        for side in (0, 2):
            @on_side(side)
            def _():
                await_coarse(side, base + n + 1)
    state = [ybuf[m] for m in range(2)]
    for n in range(lc):
        out = coarse_step(state, amps[n][0])
        for m in range(2):
            fresh = out[m][crow : 2 * crow]
            new_ref[n, m] = fresh
            gain = fresh - prev_ref[n, m]
            for part in range(4):
                pbuf[n, pl.ds(m * rows + part, crow, stride=4), :] = gain
        if n < lc - 1:
            state = following(out, base + n + 1)

    for what in range(3):
        for side in (0, 2):
            @on_side(side)
            def _():
                near(what, side).wait_send()

    @pl.when(cut == 0)
    def _():
        each_coarse_send(0, lc, True, lambda copy: copy.wait_send())
    for n in range(lc):
        each_coarse_send(base + n + 1, n, n < lc - 1, lambda copy: copy.wait_send())


def finish(fine_ref, new_ref, pbuf, spread_ref, ends_out, new_out, total, sems):
    lc, _, rows, cols = fine_ref.shape
    copies = [pltpu.make_async_copy(new_ref, new_out, sems.at[lc])]
    copies[0].start()
    for n in range(lc):
        added = jnp.dot(pieces(pbuf[n]), spread_ref[...], preferred_element_type=F32)
        total[n] = fine_ref[n] + added.reshape(2, rows, cols)
        copies.append(pltpu.make_async_copy(total.at[n], ends_out.at[n], sems.at[n]))
        copies[-1].start()
    for copy in copies:
        copy.wait()


def solution(mesh):
    cuts, nsub = mesh.shape["cuts"], mesh.shape["sub"]
    tiles = mesh.shape["space"] * nsub

    def local(starts, coarse_prev, zone_ids, materials, current, bounds):
        lc, _, rows, cols = starts.shape
        crow, ccol = rows // 4, cols // 4
        half = max(4, lc)
        slices = lc * cuts
        sizes = (cuts, nsub, tiles, lc, rows, cols, materials.shape[1], half)
        vmem = pl.BlockSpec(memory_space=pltpu.VMEM)
        hbm = pl.BlockSpec(memory_space=pltpu.HBM)
        fine, new, risen, spread = pl.pallas_call(
            functools.partial(kernel, sizes),
            out_shape=(
                jax.ShapeDtypeStruct(starts.shape, F32),
                jax.ShapeDtypeStruct(coarse_prev.shape, F32),
                jax.ShapeDtypeStruct((lc, 2 * rows, ccol), F32),
                jax.ShapeDtypeStruct((2 * ccol, cols), BF16),
            ),
            in_specs=[hbm] * 6,
            out_specs=(vmem,) * 4,
            scratch_shapes=[
                pltpu.SMEM(materials.shape, F32),
                pltpu.SMEM(current.shape, jnp.int32),
                pltpu.SMEM(bounds.shape, jnp.int32),
                pltpu.VMEM((lc, 2, crow, ccol), F32),
                pltpu.VMEM((rows, cols), jnp.int32),
                pltpu.VMEM((2 * cols, ccol), BF16),
                pltpu.VMEM((lc, 2, rows + 16, cols), F32),
                pltpu.VMEM((lc, 2, rows + 16, cols), F32),
                pltpu.VMEM((2, rows + 16, cols), F32),
                pltpu.VMEM((4, rows, cols), F32),
                pltpu.VMEM((2, 5, rows, cols), F32),
                pltpu.VMEM((3, rows, cols), F32),
                pltpu.VMEM((8, cols), jnp.int32),
                pltpu.VMEM((8, cols), jnp.int32),
                pltpu.VMEM((2, 2 * half, cols), F32),
                pltpu.VMEM((2, 2 * half, cols), F32),
                pltpu.VMEM((2, 2 * half, cols), F32),
                pltpu.VMEM((2, 2 * half, cols), F32),
                pltpu.VMEM((4, 3 * crow, ccol), F32),
                pltpu.VMEM((slices + 1, 2, 3 * crow, ccol), F32),
                pltpu.VMEM((4 * rows, ccol), F32),
                pltpu.VMEM((2, 3 * crow, ccol), F32),
                pltpu.SemaphoreType.DMA((6,)),
                pltpu.SemaphoreType.DMA((3, 2)),
                pltpu.SemaphoreType.DMA((3, 2)),
                pltpu.SemaphoreType.DMA((cuts, 3, lc + 1)),
                pltpu.SemaphoreType.DMA((3, slices + 1)),
            ],
            compiler_params=pltpu.CompilerParams(
                collective_id=0, has_side_effects=True, vmem_limit_bytes=32 * 1024 * 1024
            ),
        )(*(
            pltpu.with_memory_space_constraint(given, pltpu.HBM)
            for given in (starts, coarse_prev, zone_ids, materials, current, bounds)
        ))
        return pl.pallas_call(
            finish,
            out_shape=(
                jax.ShapeDtypeStruct(starts.shape, F32),
                jax.ShapeDtypeStruct(coarse_prev.shape, F32),
            ),
            in_specs=[vmem] * 4,
            out_specs=(hbm, hbm),
            scratch_shapes=[
                pltpu.VMEM(starts.shape, F32),
                pltpu.SemaphoreType.DMA((lc + 1,)),
            ],
            compiler_params=pltpu.CompilerParams(vmem_limit_bytes=16 * 1024 * 1024),
        )(fine, new, risen, spread)

    placed = (
        P(("grp", "cuts"), None, ("space", "sub"), None),
        P(("grp", "cuts"), None, ("space", "sub"), None),
        P(("grp", "space", "sub"), None),
        P(),
        P("grp"),
        P(),
    )
    return jax.shard_map(
        local,
        mesh=mesh,
        in_specs=placed,
        out_specs=(
            P(("grp", "cuts"), None, ("space", "sub"), None),
            P(("grp", "cuts"), None, ("space", "sub"), None),
        ),
        check_vma=False,
    )
```

```python
import functools
import jax
import jax.numpy as jnp
from jax import lax
from jax.experimental import pallas as pl
from jax.experimental.pallas import tpu as pltpu
from jax.sharding import PartitionSpec as P

JOULE_GAIN = 0.5
MESH = pl.DeviceIdType.MESH
F32 = jnp.float32
BF16 = jnp.bfloat16


def pieces(values):
    high = values.astype(BF16)
    low = (values - high.astype(F32)).astype(BF16)
    return jnp.concatenate([high, low], axis=1)


def advance(sums, turn_amps, keep, mix):
    change = sums[0][1] + turn_amps
    magnet = sums[0][0] + change
    thermal = sums[1][0] + sums[1][1] + JOULE_GAIN * change * change
    return keep * magnet + mix * thermal, mix * magnet + keep * thermal


def link_factors(coupling, span):
    coupled = span * coupling
    diagonal = 1.0 + coupled
    offdiag = 0.5 * coupled
    determinant = diagonal * diagonal - offdiag * offdiag
    return diagonal / determinant, offdiag / determinant


def kernel(
    sizes, starts_hbm, prev_hbm, zone_hbm, mat_hbm, current_hbm, bounds_hbm,
    ends_ref, new_ref, pbuf, spread_ref,
    mat_ref, current_ref, bounds_ref, prev_ref, zone_ref, gather_ref, s0, s1, rf, fl, wt, pqs, zt, zb, mu, md, ht, hb, cf, grid_c, tbuf, ybuf,
    in_sem, send_near, recv_near, send_c, recv_c,
):
    cuts, nsub, tiles, lc, rows, cols, zones, half = sizes
    crow, ccol = rows // 4, cols // 4
    chunks = rows // 8
    cut = lax.axis_index("cuts")
    tile = lax.axis_index("space") * nsub + lax.axis_index("sub")
    has_up = tile > 0
    has_down = tile < tiles - 1
    base = cut * lc

    def where_is(side, cut_no=None):
        other = tile + (side - 1)
        place = {"space": lax.div(other, nsub), "sub": lax.rem(other, nsub)}
        if cut_no is not None:
            place["cuts"] = cut_no
        return place

    def on_side(side):
        if side == 1:
            return lambda fn: fn()
        return pl.when(has_up if side == 0 else has_down)

    small = [
        pltpu.make_async_copy(source, target, in_sem.at[3 + k])
        for k, (source, target) in enumerate(
            ((mat_hbm, mat_ref), (current_hbm, current_ref), (bounds_hbm, bounds_ref))
        )
    ]
    for copy in small:
        copy.start()
    loads = [
        pltpu.make_async_copy(
            starts_hbm.at[:, :, pl.ds(first, count), :],
            s0.at[:, :, pl.ds(8 + first, count), :],
            in_sem.at[place],
        )
        for first, count, place in ((0, 8, 0), (rows - 8, 8, 6), (8, rows - 16, 7))
    ]
    for copy in loads:
        copy.start()
    load_zone = pltpu.make_async_copy(zone_hbm, zone_ref, in_sem.at[1])
    load_zone.start()
    load_prev = pltpu.make_async_copy(prev_hbm, prev_ref, in_sem.at[2])
    load_prev.start()

    barrier = pltpu.get_barrier_semaphore()
    for side in (0, 2):
        @on_side(side)
        def _():
            pl.semaphore_signal(barrier, inc=1, device_id=where_is(side), device_id_type=MESH)
    for step in range(1, cuts):
        other_cut = lax.rem(cut + step, cuts)
        for side in range(3):
            @on_side(side)
            def _():
                pl.semaphore_signal(
                    barrier, inc=1, device_id=where_is(side, other_cut), device_id_type=MESH
                )

    row8 = lax.broadcasted_iota(jnp.int32, (8, cols), 0)
    col8 = lax.broadcasted_iota(jnp.int32, (8, cols), 1)
    rowh = lax.broadcasted_iota(jnp.int32, (2 * half, cols), 0)
    colh = lax.broadcasted_iota(jnp.int32, (2 * half, cols), 1)

    def lookup(zone):
        found = [jnp.full(zone.shape, mat_ref[m, 0], F32) for m in range(4)]
        for zone_no in range(1, zones):
            present = zone == zone_no
            found = [jnp.where(present, mat_ref[m, zone_no], found[m]) for m in range(4)]
        return found

    def restricted(values, buf):
        count = values.shape[0]
        buf[0:count, :] = jnp.dot(
            pieces(values), gather_ref[...], preferred_element_type=F32
        )
        total = buf[pl.ds(0, count // 4, stride=4), :]
        for part in range(1, 4):
            total = total + buf[pl.ds(part, count // 4, stride=4), :]
        return total

    loads[0].wait()
    loads[1].wait()
    if lc < half:
        mu[...] = jnp.zeros(mu.shape, F32)
        md[...] = jnp.zeros(md.shape, F32)
    for n in range(lc):
        for m in range(2):
            mu[m, half + n : half + n + 1, :] = s0[n, m, 8:9, :]
            mu[m, n : n + 1, :] = s0[n, m, 9:10, :]
            md[m, n : n + 1, :] = s0[n, m, rows + 7 : rows + 8, :]
            md[m, half + n : half + n + 1, :] = s0[n, m, rows + 6 : rows + 7, :]

    ups = jnp.where(has_up, 1, 0) + jnp.where(has_down, 1, 0)
    pl.semaphore_wait(barrier, ups + (cuts - 1) * (1 + ups))

    def near(what, side):
        if what == 0:
            source = zone_hbm.at[0:8] if side == 0 else zone_hbm.at[rows - 8 : rows]
            target = zb if side == 0 else zt
        elif what == 1:
            source = mu if side == 0 else md
            target = hb if side == 0 else ht
        else:
            source = cf.at[:, pl.ds(crow, crow), :]
            target = cf.at[:, pl.ds(2 * crow if side == 0 else 0, crow), :]
        return pltpu.make_async_remote_copy(
            src_ref=source,
            dst_ref=target,
            send_sem=send_near.at[what, side // 2],
            recv_sem=recv_near.at[what, side // 2],
            device_id=where_is(side),
            device_id_type=MESH,
        )

    def coarse_copy(side, first, count, mark, kind, dest):
        return pltpu.make_async_remote_copy(
            src_ref=grid_c.at[pl.ds(first, count), :, pl.ds(crow, crow), :],
            dst_ref=grid_c.at[pl.ds(first, count), :, pl.ds((2 - side) * crow, crow), :],
            send_sem=send_c.at[dest, side, kind],
            recv_sem=recv_c.at[2 - side, mark],
            device_id=where_is(side, None if dest == 0 else dest),
            device_id_type=MESH,
        )

    def each_coarse_send(first, count, mark, kind, action):
        for side in (0, 2):
            @on_side(side)
            def _():
                action(coarse_copy(side, first, count, mark, kind, 0))
        for dest in range(1, cuts):
            @pl.when(cut < dest)
            def _():
                for side in (1, 0, 2):
                    @on_side(side)
                    def _():
                        action(coarse_copy(side, first, count, mark, kind, dest))

    def await_coarse(side, first, count, mark):
        pltpu.make_async_remote_copy(
            src_ref=grid_c.at[pl.ds(first, count), :, pl.ds(crow, crow), :],
            dst_ref=grid_c.at[pl.ds(first, count), :, pl.ds(side * crow, crow), :],
            send_sem=send_c.at[0, 0, 0],
            recv_sem=recv_c.at[side, mark],
            device_id=where_is(1, lax.rem(cut + 1, cuts)),
            device_id_type=MESH,
        ).wait_recv()

    for what in (0, 1):
        for side in (0, 2):
            @on_side(side)
            def _():
                near(what, side).start()
    for copy in small:
        copy.wait()

    @pl.when(jnp.logical_not(has_up))
    def _():
        zt[...] = jnp.zeros(zt.shape, jnp.int32)
        ht[...] = jnp.zeros(ht.shape, F32)
        for m in range(4):
            cf[m, 0:crow, :] = jnp.full((crow, ccol), mat_ref[m, 0], F32)
        grid_c[:, :, 0:crow, :] = jnp.zeros(grid_c.shape[:2] + (crow, ccol), F32)

    @pl.when(jnp.logical_not(has_down))
    def _():
        zb[...] = jnp.zeros(zb.shape, jnp.int32)
        hb[...] = jnp.zeros(hb.shape, F32)
        for m in range(4):
            cf[m, 2 * crow : 3 * crow, :] = jnp.full((crow, ccol), mat_ref[m, 0], F32)
        grid_c[:, :, 2 * crow : 3 * crow, :] = jnp.zeros(grid_c.shape[:2] + (crow, ccol), F32)

    tall_row = lax.broadcasted_iota(jnp.int32, (cols, ccol), 0)
    tall_col = lax.broadcasted_iota(jnp.int32, (cols, ccol), 1)
    wide_row = lax.broadcasted_iota(jnp.int32, (ccol, cols), 0)
    wide_col = lax.broadcasted_iota(jnp.int32, (ccol, cols), 1)
    gather = jnp.where((tall_row >> 2) == tall_col, 0.0625, 0.0).astype(BF16)
    spread = jnp.where((wide_col >> 2) == wide_row, 1.0, 0.0).astype(BF16)
    for part in range(2):
        gather_ref[part * cols : (part + 1) * cols, :] = gather
        spread_ref[part * ccol : (part + 1) * ccol, :] = spread

    load_zone.wait()
    for i in range(chunks):
        found = lookup(zone_ref[8 * i : 8 * i + 8, :])
        for m in range(4):
            fl[m, 8 * i : 8 * i + 8, :] = found[m]
        for m in range(2):
            rf[m, 8 + 8 * i : 16 + 8 * i, :] = found[m]
        keep, mix = link_factors(found[2], 1.0)
        pqs[0, 8 * i : 8 * i + 8, :] = keep
        pqs[1, 8 * i : 8 * i + 8, :] = mix
        pqs[2, 8 * i : 8 * i + 8, :] = found[3]

    own_c = restricted(fl[...].reshape(4 * rows, cols), tbuf)
    for m in range(4):
        cf[m, crow : 2 * crow, :] = own_c[m * crow : (m + 1) * crow]
    for side in (0, 2):
        @on_side(side)
        def _():
            near(2, side).start()

    loads[2].wait()

    @pl.when(cut == 0)
    def _():
        first = restricted(s0[0, :, 8 : 8 + rows, :].reshape(2 * rows, cols), tbuf)
        for m in range(2):
            grid_c[0, m, crow : 2 * crow, :] = first[m * crow : (m + 1) * crow]
        each_coarse_send(0, 1, 0, 0, lambda copy: copy.start())

    def lateral(value, edge, col):
        width = value.shape[1]
        left = jnp.where(col == 0, edge, pltpu.roll(value, 1, 1))
        right = jnp.where(col == width - 1, edge, pltpu.roll(value, width - 1, 1))
        return 0.5 * (value + left), 0.5 * (value + right)

    def five(center, up, down, edge, col):
        west, east = lateral(center, edge, col)
        north = 0.5 * (center + up)
        south = 0.5 * (center + down)
        width = center.shape[1]
        return (
            jnp.where(col == width - 1, 0.0, east),
            jnp.where(col == 0, 0.0, west),
            north,
            south,
            (west + east) + (north + south),
        )

    def make_weights(i):
        low = 8 + 8 * i
        for m in range(2):
            made = five(
                rf[m, low : low + 8, :], rf[m, low - 1 : low + 7, :],
                rf[m, low + 1 : low + 9, :], mat_ref[m, 0], col8,
            )
            for k in range(5):
                wt[m, k, 8 * i : 8 * i + 8, :] = made[k]

    def spread_sum(weights, center, up, down):
        width = center.shape[1]
        east, west, north, south, whole = weights
        total = east * pltpu.roll(center, width - 1, 1) + west * pltpu.roll(center, 1, 1)
        return (total + (north * up + south * down)) - whole * center

    def amps_at(slice_no, offset):
        return current_ref[bounds_ref[slice_no] + offset].astype(F32) * 0.001

    amps = [[amps_at(base + n, j) for j in range(2)] for n in range(lc)]

    def fine_chunk(source, n, i, amperes):
        low = 8 + 8 * i
        at = slice(8 * i, 8 * i + 8)
        sums = []
        for m in range(2):
            center = source[n, m, low : low + 8, :]
            weights = [wt[m, k, at, :] for k in range(5)]
            sums.append((center, spread_sum(
                weights, center, source[n, m, low - 1 : low + 7, :],
                source[n, m, low + 1 : low + 9, :],
            )))
        return advance(sums, pqs[2, at, :] * amperes, pqs[0, at, :], pqs[1, at, :])

    def first_step(n, i):
        out = fine_chunk(s0, n, i, amps[n][0])
        for m in range(2):
            s1[n, m, 8 + 8 * i : 16 + 8 * i, :] = out[m]

    for i in range(1, chunks - 1):
        make_weights(i)
    for n in range(lc):
        for i in range(1, chunks - 1):
            first_step(n, i)

    for side in (0, 2):
        @on_side(side)
        def _():
            near(0, 2 - side).wait_recv()
    above = lookup(zt[...])
    below = lookup(zb[...])
    for m in range(2):
        rf[m, 0:8, :] = above[m]
        rf[m, rows + 8 : rows + 16, :] = below[m]

    for i in (0, chunks - 1):
        make_weights(i)

    def both(top, bottom):
        shape = (2 * half, cols)
        return jnp.where(rowh < half, jnp.broadcast_to(top, shape), jnp.broadcast_to(bottom, shape))

    edge_weights = []
    for m in range(2):
        center = both(rf[m, 7:8, :], rf[m, rows + 8 : rows + 9, :])
        outer = both(rf[m, 6:7, :], rf[m, rows + 9 : rows + 10, :])
        inner = both(rf[m, 8:9, :], rf[m, rows + 7 : rows + 8, :])
        edge_weights.append(five(center, outer, inner, mat_ref[m, 0], colh))
    edge_keep, edge_mix = link_factors(both(above[2][7:8], below[2][0:1]), 1.0)
    edge_amps = jnp.zeros((2 * half, cols), F32)
    for n in range(lc):
        edge_amps = jnp.where(
            jnp.logical_or(rowh == n, rowh == half + n), amps[n][0], edge_amps
        )
    edge_turn = both(above[3][7:8], below[3][0:1]) * edge_amps

    for side in (0, 2):
        @on_side(side)
        def _():
            near(1, 2 - side).wait_recv()

    edge_sums = []
    for m in range(2):
        center = jnp.where(rowh < half, ht[m], hb[m])
        outer = pltpu.roll(jnp.where(rowh < half, hb[m], ht[m]), half, 0)
        inner = pltpu.roll(jnp.where(rowh < half, md[m], mu[m]), half, 0)
        edge_sums.append((center, spread_sum(edge_weights[m], center, outer, inner)))
        for n in range(lc):
            s0[n, m, 7:8, :] = ht[m, n : n + 1, :]
            s0[n, m, rows + 8 : rows + 9, :] = hb[m, half + n : half + n + 1, :]
    edge_out = advance(edge_sums, edge_turn, edge_keep, edge_mix)
    inside = jnp.where(
        rowh < half, jnp.where(has_up, 1, 0), jnp.where(has_down, 1, 0)
    ) > 0
    for m in range(2):
        kept = jnp.where(inside, edge_out[m], 0.0)
        for n in range(lc):
            s1[n, m, 7:8, :] = kept[n : n + 1]
            s1[n, m, rows + 8 : rows + 9, :] = kept[half + n : half + n + 1]

    load_prev.wait()
    for n in range(lc):
        for i in (0, chunks - 1):
            first_step(n, i)
        for i in range(chunks):
            out = fine_chunk(s1, n, i, amps[n][1])
            for m in range(2):
                ends_ref[n, m, 8 * i : 8 * i + 8, :] = out[m]
        mean = restricted(ends_ref[n].reshape(2 * rows, cols), tbuf)
        for m in range(2):
            grid_c[base + n + 1, m, crow : 2 * crow, :] = (
                mean[m * crow : (m + 1) * crow] - prev_ref[n, m]
            )
    each_coarse_send(base + 1, lc, cut + 1, 1, lambda copy: copy.start())

    for side in (0, 2):
        @on_side(side)
        def _():
            near(2, 2 - side).wait_recv()
    tall = 3 * crow
    crows = lax.broadcasted_iota(jnp.int32, (tall, ccol), 0)
    ccols = lax.broadcasted_iota(jnp.int32, (tall, ccol), 1)
    in_grid = jnp.logical_and(
        jnp.where(crows < crow, jnp.where(has_up, 1, 0), 1) > 0,
        jnp.where(crows >= 2 * crow, jnp.where(has_down, 1, 0), 1) > 0,
    )
    coarse_weights = []
    for m in range(2):
        center = cf[m] * 0.125
        coarse_weights.append(five(
            center, pltpu.roll(center, 1, 0), pltpu.roll(center, tall - 1, 0),
            mat_ref[m, 0] * 0.125, ccols,
        ))
    coarse_keep, coarse_mix = link_factors(cf[2], 2.0)
    coarse_turn = 2.0 * cf[3]

    def coarse_step(state, amperes):
        sums = []
        for m in range(2):
            center = state[m]
            sums.append((center, spread_sum(
                coarse_weights[m], center, pltpu.roll(center, 1, 0),
                pltpu.roll(center, tall - 1, 0),
            )))
        return advance(sums, coarse_turn * amperes, coarse_keep, coarse_mix)

    def following(out, g):
        return [jnp.where(in_grid, out[m] + grid_c[g, m], 0.0) for m in range(2)]

    @pl.when(cut > 0)
    def _():
        await_coarse(1, 0, 1, 0)
    for side in (0, 2):
        @on_side(side)
        def _():
            await_coarse(side, 0, 1, 0)
    for m in range(2):
        ybuf[m] = grid_c[0, m]
    for before in range(cuts - 1):
        @pl.when(cut > before)
        def _():
            for side in range(3):
                @on_side(side)
                def _():
                    await_coarse(side, before * lc + 1, lc, before + 1)
            state = [ybuf[m] for m in range(2)]
            for n in range(lc):
                slice_no = before * lc + n
                out = coarse_step(state, amps_at(slice_no, 0))
                state = following(out, slice_no + 1)
            for m in range(2):
                ybuf[m] = state[m]

    for side in (0, 2):
        @on_side(side)
        def _():
            await_coarse(side, base + 1, lc, cut + 1)
    state = [ybuf[m] for m in range(2)]
    for n in range(lc):
        out = coarse_step(state, amps[n][0])
        for m in range(2):
            fresh = out[m][crow : 2 * crow]
            new_ref[n, m] = fresh
            gain = fresh - prev_ref[n, m]
            for part in range(4):
                pbuf[n, pl.ds(m * rows + part, crow, stride=4), :] = gain
        if n < lc - 1:
            state = following(out, base + n + 1)

    for what in range(3):
        for side in (0, 2):
            @on_side(side)
            def _():
                near(what, side).wait_send()

    @pl.when(cut == 0)
    def _():
        each_coarse_send(0, 1, 0, 0, lambda copy: copy.wait_send())
    each_coarse_send(base + 1, lc, cut + 1, 1, lambda copy: copy.wait_send())


def finish(fine_ref, new_ref, pbuf, spread_ref, ends_out, new_out, total, sems):
    lc, _, rows, cols = fine_ref.shape
    copies = [pltpu.make_async_copy(new_ref, new_out, sems.at[lc])]
    copies[0].start()
    for n in range(lc):
        added = jnp.dot(pieces(pbuf[n]), spread_ref[...], preferred_element_type=F32)
        total[n] = fine_ref[n] + added.reshape(2, rows, cols)
        copies.append(pltpu.make_async_copy(total.at[n], ends_out.at[n], sems.at[n]))
        copies[-1].start()
    for copy in copies:
        copy.wait()


def solution(mesh):
    cuts, nsub = mesh.shape["cuts"], mesh.shape["sub"]
    tiles = mesh.shape["space"] * nsub

    def local(starts, coarse_prev, zone_ids, materials, current, bounds):
        lc, _, rows, cols = starts.shape
        crow, ccol = rows // 4, cols // 4
        half = max(4, lc)
        slices = lc * cuts
        sizes = (cuts, nsub, tiles, lc, rows, cols, materials.shape[1], half)
        vmem = pl.BlockSpec(memory_space=pltpu.VMEM)
        hbm = pl.BlockSpec(memory_space=pltpu.HBM)
        fine, new, risen, spread = pl.pallas_call(
            functools.partial(kernel, sizes),
            out_shape=(
                jax.ShapeDtypeStruct(starts.shape, F32),
                jax.ShapeDtypeStruct(coarse_prev.shape, F32),
                jax.ShapeDtypeStruct((lc, 2 * rows, ccol), F32),
                jax.ShapeDtypeStruct((2 * ccol, cols), BF16),
            ),
            in_specs=[hbm] * 6,
            out_specs=(vmem,) * 4,
            scratch_shapes=[
                pltpu.SMEM(materials.shape, F32),
                pltpu.SMEM(current.shape, jnp.int32),
                pltpu.SMEM(bounds.shape, jnp.int32),
                pltpu.VMEM((lc, 2, crow, ccol), F32),
                pltpu.VMEM((rows, cols), jnp.int32),
                pltpu.VMEM((2 * cols, ccol), BF16),
                pltpu.VMEM((lc, 2, rows + 16, cols), F32),
                pltpu.VMEM((lc, 2, rows + 16, cols), F32),
                pltpu.VMEM((2, rows + 16, cols), F32),
                pltpu.VMEM((4, rows, cols), F32),
                pltpu.VMEM((2, 5, rows, cols), F32),
                pltpu.VMEM((3, rows, cols), F32),
                pltpu.VMEM((8, cols), jnp.int32),
                pltpu.VMEM((8, cols), jnp.int32),
                pltpu.VMEM((2, 2 * half, cols), F32),
                pltpu.VMEM((2, 2 * half, cols), F32),
                pltpu.VMEM((2, 2 * half, cols), F32),
                pltpu.VMEM((2, 2 * half, cols), F32),
                pltpu.VMEM((4, 3 * crow, ccol), F32),
                pltpu.VMEM((slices + 1, 2, 3 * crow, ccol), F32),
                pltpu.VMEM((4 * rows, ccol), F32),
                pltpu.VMEM((2, 3 * crow, ccol), F32),
                pltpu.SemaphoreType.DMA((8,)),
                pltpu.SemaphoreType.DMA((3, 2)),
                pltpu.SemaphoreType.DMA((3, 2)),
                pltpu.SemaphoreType.DMA((cuts, 3, 2)),
                pltpu.SemaphoreType.DMA((3, cuts + 1)),
            ],
            compiler_params=pltpu.CompilerParams(
                collective_id=0, has_side_effects=True, vmem_limit_bytes=32 * 1024 * 1024
            ),
        )(*(
            pltpu.with_memory_space_constraint(given, pltpu.HBM)
            for given in (starts, coarse_prev, zone_ids, materials, current, bounds)
        ))
        return pl.pallas_call(
            finish,
            out_shape=(
                jax.ShapeDtypeStruct(starts.shape, F32),
                jax.ShapeDtypeStruct(coarse_prev.shape, F32),
            ),
            in_specs=[vmem] * 4,
            out_specs=(hbm, hbm),
            scratch_shapes=[
                pltpu.VMEM(starts.shape, F32),
                pltpu.SemaphoreType.DMA((lc + 1,)),
            ],
            compiler_params=pltpu.CompilerParams(vmem_limit_bytes=16 * 1024 * 1024),
        )(fine, new, risen, spread)

    placed = (
        P(("grp", "cuts"), None, ("space", "sub"), None),
        P(("grp", "cuts"), None, ("space", "sub"), None),
        P(("grp", "space", "sub"), None),
        P(),
        P("grp"),
        P(),
    )
    return jax.shard_map(
        local,
        mesh=mesh,
        in_specs=placed,
        out_specs=(
            P(("grp", "cuts"), None, ("space", "sub"), None),
            P(("grp", "cuts"), None, ("space", "sub"), None),
        ),
        check_vma=False,
    )
```

```python
import functools
import jax
import jax.numpy as jnp
from jax import lax
from jax.experimental import pallas as pl
from jax.experimental.pallas import tpu as pltpu
from jax.sharding import PartitionSpec as P

JOULE_GAIN = 0.5
MESH = pl.DeviceIdType.MESH
F32 = jnp.float32
BF16 = jnp.bfloat16


def pieces(values):
    high = values.astype(BF16)
    low = (values - high.astype(F32)).astype(BF16)
    return jnp.concatenate([high, low], axis=1)


def advance(sums, turn_amps, keep, mix):
    change = sums[0][1] + turn_amps
    magnet = sums[0][0] + change
    thermal = sums[1][0] + sums[1][1] + JOULE_GAIN * change * change
    return keep * magnet + mix * thermal, mix * magnet + keep * thermal


def link_factors(coupling, span):
    coupled = span * coupling
    diagonal = 1.0 + coupled
    offdiag = 0.5 * coupled
    determinant = diagonal * diagonal - offdiag * offdiag
    return diagonal / determinant, offdiag / determinant


def kernel(
    sizes, starts_hbm, prev_hbm, zone_hbm, mat_hbm, current_hbm, bounds_hbm,
    ends_ref, new_ref, pbuf, spread_ref,
    mat_ref, current_ref, bounds_ref, prev_ref, zone_ref, gather_ref, s0, s1, rf, fl, wt, pqs, zt, zb, mu, md, ht, hb, cf, grid_c, tbuf, ybuf,
    in_sem, send_near, recv_near, send_c, recv_c,
):
    cuts, nsub, tiles, lc, rows, cols, zones, half = sizes
    crow, ccol = rows // 4, cols // 4
    chunks = rows // 8
    cut = lax.axis_index("cuts")
    tile = lax.axis_index("space") * nsub + lax.axis_index("sub")
    has_up = tile > 0
    has_down = tile < tiles - 1
    base = cut * lc

    def where_is(side, cut_no=None):
        other = tile + (side - 1)
        place = {"space": lax.div(other, nsub), "sub": lax.rem(other, nsub)}
        if cut_no is not None:
            place["cuts"] = cut_no
        return place

    def on_side(side):
        if side == 1:
            return lambda fn: fn()
        return pl.when(has_up if side == 0 else has_down)

    load_zone = pltpu.make_async_copy(zone_hbm, zone_ref, in_sem.at[1])
    load_zone.start()
    small = [
        pltpu.make_async_copy(source, target, in_sem.at[3 + k])
        for k, (source, target) in enumerate(
            ((mat_hbm, mat_ref), (current_hbm, current_ref), (bounds_hbm, bounds_ref))
        )
    ]
    for copy in small:
        copy.start()
    load = pltpu.make_async_copy(starts_hbm, s0.at[:, :, pl.ds(8, rows), :], in_sem.at[0])
    load.start()
    load_prev = pltpu.make_async_copy(prev_hbm, prev_ref, in_sem.at[2])
    load_prev.start()

    barrier = pltpu.get_barrier_semaphore()
    for side in (0, 2):
        @on_side(side)
        def _():
            pl.semaphore_signal(barrier, inc=1, device_id=where_is(side), device_id_type=MESH)
    for step in range(1, cuts):
        other_cut = lax.rem(cut + step, cuts)
        for side in range(3):
            @on_side(side)
            def _():
                pl.semaphore_signal(
                    barrier, inc=1, device_id=where_is(side, other_cut), device_id_type=MESH
                )

    row8 = lax.broadcasted_iota(jnp.int32, (8, cols), 0)
    col8 = lax.broadcasted_iota(jnp.int32, (8, cols), 1)
    rowh = lax.broadcasted_iota(jnp.int32, (2 * half, cols), 0)
    colh = lax.broadcasted_iota(jnp.int32, (2 * half, cols), 1)

    def lookup(zone):
        found = [jnp.full(zone.shape, mat_ref[m, 0], F32) for m in range(4)]
        for zone_no in range(1, zones):
            present = zone == zone_no
            found = [jnp.where(present, mat_ref[m, zone_no], found[m]) for m in range(4)]
        return found

    def restricted(values, buf):
        count = values.shape[0]
        buf[0:count, :] = jnp.dot(
            pieces(values), gather_ref[...], preferred_element_type=F32
        )
        total = buf[pl.ds(0, count // 4, stride=4), :]
        for part in range(1, 4):
            total = total + buf[pl.ds(part, count // 4, stride=4), :]
        return total

    tall_row = lax.broadcasted_iota(jnp.int32, (cols, ccol), 0)
    tall_col = lax.broadcasted_iota(jnp.int32, (cols, ccol), 1)
    wide_row = lax.broadcasted_iota(jnp.int32, (ccol, cols), 0)
    wide_col = lax.broadcasted_iota(jnp.int32, (ccol, cols), 1)
    gather = jnp.where((tall_row >> 2) == tall_col, 0.0625, 0.0).astype(BF16)
    spread = jnp.where((wide_col >> 2) == wide_row, 1.0, 0.0).astype(BF16)
    for part in range(2):
        gather_ref[part * cols : (part + 1) * cols, :] = gather
        spread_ref[part * ccol : (part + 1) * ccol, :] = spread

    for copy in small:
        copy.wait()
    load_zone.wait()
    for i in range(chunks):
        found = lookup(zone_ref[8 * i : 8 * i + 8, :])
        for m in range(4):
            fl[m, 8 * i : 8 * i + 8, :] = found[m]
        for m in range(2):
            rf[m, 8 + 8 * i : 16 + 8 * i, :] = found[m]
        keep, mix = link_factors(found[2], 1.0)
        pqs[0, 8 * i : 8 * i + 8, :] = keep
        pqs[1, 8 * i : 8 * i + 8, :] = mix
        pqs[2, 8 * i : 8 * i + 8, :] = found[3]

    load.wait()
    if lc < half:
        mu[...] = jnp.zeros(mu.shape, F32)
        md[...] = jnp.zeros(md.shape, F32)
    for n in range(lc):
        for m in range(2):
            mu[m, half + n : half + n + 1, :] = s0[n, m, 8:9, :]
            mu[m, n : n + 1, :] = s0[n, m, 9:10, :]
            md[m, n : n + 1, :] = s0[n, m, rows + 7 : rows + 8, :]
            md[m, half + n : half + n + 1, :] = s0[n, m, rows + 6 : rows + 7, :]

    def lateral(value, edge, col):
        width = value.shape[1]
        left = jnp.where(col == 0, edge, pltpu.roll(value, 1, 1))
        right = jnp.where(col == width - 1, edge, pltpu.roll(value, width - 1, 1))
        return 0.5 * (value + left), 0.5 * (value + right)

    def five(center, up, down, edge, col):
        west, east = lateral(center, edge, col)
        north = 0.5 * (center + up)
        south = 0.5 * (center + down)
        width = center.shape[1]
        return (
            jnp.where(col == width - 1, 0.0, east),
            jnp.where(col == 0, 0.0, west),
            north,
            south,
            (west + east) + (north + south),
        )

    def make_weights(i):
        low = 8 + 8 * i
        for m in range(2):
            made = five(
                rf[m, low : low + 8, :], rf[m, low - 1 : low + 7, :],
                rf[m, low + 1 : low + 9, :], mat_ref[m, 0], col8,
            )
            for k in range(5):
                wt[m, k, 8 * i : 8 * i + 8, :] = made[k]

    def spread_sum(weights, center, up, down):
        width = center.shape[1]
        east, west, north, south, whole = weights
        total = east * pltpu.roll(center, width - 1, 1) + west * pltpu.roll(center, 1, 1)
        return (total + (north * up + south * down)) - whole * center

    def amps_at(slice_no, offset):
        return current_ref[bounds_ref[slice_no] + offset].astype(F32) * 0.001

    amps = [[amps_at(base + n, j) for j in range(2)] for n in range(lc)]

    def fine_chunk(source, n, i, amperes):
        low = 8 + 8 * i
        at = slice(8 * i, 8 * i + 8)
        sums = []
        for m in range(2):
            center = source[n, m, low : low + 8, :]
            weights = [wt[m, k, at, :] for k in range(5)]
            sums.append((center, spread_sum(
                weights, center, source[n, m, low - 1 : low + 7, :],
                source[n, m, low + 1 : low + 9, :],
            )))
        return advance(sums, pqs[2, at, :] * amperes, pqs[0, at, :], pqs[1, at, :])

    def first_step(n, i):
        out = fine_chunk(s0, n, i, amps[n][0])
        for m in range(2):
            s1[n, m, 8 + 8 * i : 16 + 8 * i, :] = out[m]

    for i in range(1, chunks - 1):
        make_weights(i)
    for n in range(lc):
        for i in range(1, chunks - 1):
            first_step(n, i)

    own_c = restricted(fl[...].reshape(4 * rows, cols), tbuf)
    for m in range(4):
        cf[m, crow : 2 * crow, :] = own_c[m * crow : (m + 1) * crow]
    ups = jnp.where(has_up, 1, 0) + jnp.where(has_down, 1, 0)
    pl.semaphore_wait(barrier, ups + (cuts - 1) * (1 + ups))

    def near(what, side):
        if what == 0:
            source = zone_ref.at[0:8] if side == 0 else zone_ref.at[rows - 8 : rows]
            target = zb if side == 0 else zt
        elif what == 1:
            source = mu if side == 0 else md
            target = hb if side == 0 else ht
        else:
            source = cf.at[:, pl.ds(crow, crow), :]
            target = cf.at[:, pl.ds(2 * crow if side == 0 else 0, crow), :]
        return pltpu.make_async_remote_copy(
            src_ref=source,
            dst_ref=target,
            send_sem=send_near.at[what, side // 2],
            recv_sem=recv_near.at[what, side // 2],
            device_id=where_is(side),
            device_id_type=MESH,
        )

    def coarse_copy(side, first, count, mark, kind, dest):
        return pltpu.make_async_remote_copy(
            src_ref=grid_c.at[pl.ds(first, count), :, pl.ds(crow, crow), :],
            dst_ref=grid_c.at[pl.ds(first, count), :, pl.ds((2 - side) * crow, crow), :],
            send_sem=send_c.at[dest, side, kind],
            recv_sem=recv_c.at[2 - side, mark],
            device_id=where_is(side, None if dest == 0 else dest),
            device_id_type=MESH,
        )

    def each_coarse_send(first, count, mark, kind, action):
        for side in (0, 2):
            @on_side(side)
            def _():
                action(coarse_copy(side, first, count, mark, kind, 0))
        for dest in range(1, cuts):
            @pl.when(cut < dest)
            def _():
                for side in (1, 0, 2):
                    @on_side(side)
                    def _():
                        action(coarse_copy(side, first, count, mark, kind, dest))

    def await_coarse(side, first, count, mark):
        pltpu.make_async_remote_copy(
            src_ref=grid_c.at[pl.ds(first, count), :, pl.ds(crow, crow), :],
            dst_ref=grid_c.at[pl.ds(first, count), :, pl.ds(side * crow, crow), :],
            send_sem=send_c.at[0, 0, 0],
            recv_sem=recv_c.at[side, mark],
            device_id=where_is(1, lax.rem(cut + 1, cuts)),
            device_id_type=MESH,
        ).wait_recv()

    for what in (0, 1):
        for side in (0, 2):
            @on_side(side)
            def _():
                near(what, side).start()

    @pl.when(jnp.logical_not(has_up))
    def _():
        zt[...] = jnp.zeros(zt.shape, jnp.int32)
        ht[...] = jnp.zeros(ht.shape, F32)
        for m in range(4):
            cf[m, 0:crow, :] = jnp.full((crow, ccol), mat_ref[m, 0], F32)
        grid_c[:, :, 0:crow, :] = jnp.zeros(grid_c.shape[:2] + (crow, ccol), F32)

    @pl.when(jnp.logical_not(has_down))
    def _():
        zb[...] = jnp.zeros(zb.shape, jnp.int32)
        hb[...] = jnp.zeros(hb.shape, F32)
        for m in range(4):
            cf[m, 2 * crow : 3 * crow, :] = jnp.full((crow, ccol), mat_ref[m, 0], F32)
        grid_c[:, :, 2 * crow : 3 * crow, :] = jnp.zeros(grid_c.shape[:2] + (crow, ccol), F32)

    for side in (0, 2):
        @on_side(side)
        def _():
            near(2, side).start()

    @pl.when(cut == 0)
    def _():
        first = restricted(s0[0, :, 8 : 8 + rows, :].reshape(2 * rows, cols), tbuf)
        for m in range(2):
            grid_c[0, m, crow : 2 * crow, :] = first[m * crow : (m + 1) * crow]
        each_coarse_send(0, 1, 0, 0, lambda copy: copy.start())

    for side in (0, 2):
        @on_side(side)
        def _():
            near(0, 2 - side).wait_recv()
    above = lookup(zt[...])
    below = lookup(zb[...])
    for m in range(2):
        rf[m, 0:8, :] = above[m]
        rf[m, rows + 8 : rows + 16, :] = below[m]

    for i in (0, chunks - 1):
        make_weights(i)

    def both(top, bottom):
        shape = (2 * half, cols)
        return jnp.where(rowh < half, jnp.broadcast_to(top, shape), jnp.broadcast_to(bottom, shape))

    edge_weights = []
    for m in range(2):
        center = both(rf[m, 7:8, :], rf[m, rows + 8 : rows + 9, :])
        outer = both(rf[m, 6:7, :], rf[m, rows + 9 : rows + 10, :])
        inner = both(rf[m, 8:9, :], rf[m, rows + 7 : rows + 8, :])
        edge_weights.append(five(center, outer, inner, mat_ref[m, 0], colh))
    edge_keep, edge_mix = link_factors(both(above[2][7:8], below[2][0:1]), 1.0)
    edge_amps = jnp.zeros((2 * half, cols), F32)
    for n in range(lc):
        edge_amps = jnp.where(
            jnp.logical_or(rowh == n, rowh == half + n), amps[n][0], edge_amps
        )
    edge_turn = both(above[3][7:8], below[3][0:1]) * edge_amps

    for side in (0, 2):
        @on_side(side)
        def _():
            near(1, 2 - side).wait_recv()

    edge_sums = []
    for m in range(2):
        center = jnp.where(rowh < half, ht[m], hb[m])
        outer = pltpu.roll(jnp.where(rowh < half, hb[m], ht[m]), half, 0)
        inner = pltpu.roll(jnp.where(rowh < half, md[m], mu[m]), half, 0)
        edge_sums.append((center, spread_sum(edge_weights[m], center, outer, inner)))
        for n in range(lc):
            s0[n, m, 7:8, :] = ht[m, n : n + 1, :]
            s0[n, m, rows + 8 : rows + 9, :] = hb[m, half + n : half + n + 1, :]
    edge_out = advance(edge_sums, edge_turn, edge_keep, edge_mix)
    inside = jnp.where(
        rowh < half, jnp.where(has_up, 1, 0), jnp.where(has_down, 1, 0)
    ) > 0
    for m in range(2):
        kept = jnp.where(inside, edge_out[m], 0.0)
        for n in range(lc):
            s1[n, m, 7:8, :] = kept[n : n + 1]
            s1[n, m, rows + 8 : rows + 9, :] = kept[half + n : half + n + 1]

    load_prev.wait()
    for n in range(lc):
        for i in (0, chunks - 1):
            first_step(n, i)
        for i in range(chunks):
            out = fine_chunk(s1, n, i, amps[n][1])
            for m in range(2):
                ends_ref[n, m, 8 * i : 8 * i + 8, :] = out[m]
        mean = restricted(ends_ref[n].reshape(2 * rows, cols), tbuf)
        for m in range(2):
            grid_c[base + n + 1, m, crow : 2 * crow, :] = (
                mean[m * crow : (m + 1) * crow] - prev_ref[n, m]
            )
    each_coarse_send(base + 1, lc, cut + 1, 1, lambda copy: copy.start())

    for side in (0, 2):
        @on_side(side)
        def _():
            near(2, 2 - side).wait_recv()
    tall = 3 * crow
    crows = lax.broadcasted_iota(jnp.int32, (tall, ccol), 0)
    ccols = lax.broadcasted_iota(jnp.int32, (tall, ccol), 1)
    in_grid = jnp.logical_and(
        jnp.where(crows < crow, jnp.where(has_up, 1, 0), 1) > 0,
        jnp.where(crows >= 2 * crow, jnp.where(has_down, 1, 0), 1) > 0,
    )
    coarse_weights = []
    for m in range(2):
        center = cf[m] * 0.125
        coarse_weights.append(five(
            center, pltpu.roll(center, 1, 0), pltpu.roll(center, tall - 1, 0),
            mat_ref[m, 0] * 0.125, ccols,
        ))
    coarse_keep, coarse_mix = link_factors(cf[2], 2.0)
    coarse_turn = 2.0 * cf[3]

    def coarse_step(state, amperes):
        sums = []
        for m in range(2):
            center = state[m]
            sums.append((center, spread_sum(
                coarse_weights[m], center, pltpu.roll(center, 1, 0),
                pltpu.roll(center, tall - 1, 0),
            )))
        return advance(sums, coarse_turn * amperes, coarse_keep, coarse_mix)

    def following(out, g):
        return [jnp.where(in_grid, out[m] + grid_c[g, m], 0.0) for m in range(2)]

    @pl.when(cut > 0)
    def _():
        await_coarse(1, 0, 1, 0)
    for side in (0, 2):
        @on_side(side)
        def _():
            await_coarse(side, 0, 1, 0)
    for m in range(2):
        ybuf[m] = grid_c[0, m]
    for before in range(cuts - 1):
        @pl.when(cut > before)
        def _():
            for side in range(3):
                @on_side(side)
                def _():
                    await_coarse(side, before * lc + 1, lc, before + 1)
            state = [ybuf[m] for m in range(2)]
            for n in range(lc):
                slice_no = before * lc + n
                out = coarse_step(state, amps_at(slice_no, 0))
                state = following(out, slice_no + 1)
            for m in range(2):
                ybuf[m] = state[m]

    for side in (0, 2):
        @on_side(side)
        def _():
            await_coarse(side, base + 1, lc, cut + 1)
    state = [ybuf[m] for m in range(2)]
    for n in range(lc):
        out = coarse_step(state, amps[n][0])
        for m in range(2):
            fresh = out[m][crow : 2 * crow]
            new_ref[n, m] = fresh
            gain = fresh - prev_ref[n, m]
            for part in range(4):
                pbuf[n, pl.ds(m * rows + part, crow, stride=4), :] = gain
        if n < lc - 1:
            state = following(out, base + n + 1)

    for what in range(3):
        for side in (0, 2):
            @on_side(side)
            def _():
                near(what, side).wait_send()

    @pl.when(cut == 0)
    def _():
        each_coarse_send(0, 1, 0, 0, lambda copy: copy.wait_send())
    each_coarse_send(base + 1, lc, cut + 1, 1, lambda copy: copy.wait_send())


def finish(fine_ref, new_ref, pbuf, spread_ref, ends_out, new_out, total, sems):
    lc, _, rows, cols = fine_ref.shape
    copies = [pltpu.make_async_copy(new_ref, new_out, sems.at[lc])]
    copies[0].start()
    for n in range(lc):
        added = jnp.dot(pieces(pbuf[n]), spread_ref[...], preferred_element_type=F32)
        total[n] = fine_ref[n] + added.reshape(2, rows, cols)
        copies.append(pltpu.make_async_copy(total.at[n], ends_out.at[n], sems.at[n]))
        copies[-1].start()
    for copy in copies:
        copy.wait()


def solution(mesh):
    cuts, nsub = mesh.shape["cuts"], mesh.shape["sub"]
    tiles = mesh.shape["space"] * nsub

    def local(starts, coarse_prev, zone_ids, materials, current, bounds):
        lc, _, rows, cols = starts.shape
        crow, ccol = rows // 4, cols // 4
        half = max(4, lc)
        slices = lc * cuts
        sizes = (cuts, nsub, tiles, lc, rows, cols, materials.shape[1], half)
        vmem = pl.BlockSpec(memory_space=pltpu.VMEM)
        hbm = pl.BlockSpec(memory_space=pltpu.HBM)
        fine, new, risen, spread = pl.pallas_call(
            functools.partial(kernel, sizes),
            out_shape=(
                jax.ShapeDtypeStruct(starts.shape, F32),
                jax.ShapeDtypeStruct(coarse_prev.shape, F32),
                jax.ShapeDtypeStruct((lc, 2 * rows, ccol), F32),
                jax.ShapeDtypeStruct((2 * ccol, cols), BF16),
            ),
            in_specs=[hbm] * 6,
            out_specs=(vmem,) * 4,
            scratch_shapes=[
                pltpu.SMEM(materials.shape, F32),
                pltpu.SMEM(current.shape, jnp.int32),
                pltpu.SMEM(bounds.shape, jnp.int32),
                pltpu.VMEM((lc, 2, crow, ccol), F32),
                pltpu.VMEM((rows, cols), jnp.int32),
                pltpu.VMEM((2 * cols, ccol), BF16),
                pltpu.VMEM((lc, 2, rows + 16, cols), F32),
                pltpu.VMEM((lc, 2, rows + 16, cols), F32),
                pltpu.VMEM((2, rows + 16, cols), F32),
                pltpu.VMEM((4, rows, cols), F32),
                pltpu.VMEM((2, 5, rows, cols), F32),
                pltpu.VMEM((3, rows, cols), F32),
                pltpu.VMEM((8, cols), jnp.int32),
                pltpu.VMEM((8, cols), jnp.int32),
                pltpu.VMEM((2, 2 * half, cols), F32),
                pltpu.VMEM((2, 2 * half, cols), F32),
                pltpu.VMEM((2, 2 * half, cols), F32),
                pltpu.VMEM((2, 2 * half, cols), F32),
                pltpu.VMEM((4, 3 * crow, ccol), F32),
                pltpu.VMEM((slices + 1, 2, 3 * crow, ccol), F32),
                pltpu.VMEM((4 * rows, ccol), F32),
                pltpu.VMEM((2, 3 * crow, ccol), F32),
                pltpu.SemaphoreType.DMA((6,)),
                pltpu.SemaphoreType.DMA((3, 2)),
                pltpu.SemaphoreType.DMA((3, 2)),
                pltpu.SemaphoreType.DMA((cuts, 3, 2)),
                pltpu.SemaphoreType.DMA((3, cuts + 1)),
            ],
            compiler_params=pltpu.CompilerParams(
                collective_id=0, has_side_effects=True, vmem_limit_bytes=32 * 1024 * 1024
            ),
        )(*(
            pltpu.with_memory_space_constraint(given, pltpu.HBM)
            for given in (starts, coarse_prev, zone_ids, materials, current, bounds)
        ))
        return pl.pallas_call(
            finish,
            out_shape=(
                jax.ShapeDtypeStruct(starts.shape, F32),
                jax.ShapeDtypeStruct(coarse_prev.shape, F32),
            ),
            in_specs=[vmem] * 4,
            out_specs=(hbm, hbm),
            scratch_shapes=[
                pltpu.VMEM(starts.shape, F32),
                pltpu.SemaphoreType.DMA((lc + 1,)),
            ],
            compiler_params=pltpu.CompilerParams(vmem_limit_bytes=16 * 1024 * 1024),
        )(fine, new, risen, spread)

    placed = (
        P(("grp", "cuts"), None, ("space", "sub"), None),
        P(("grp", "cuts"), None, ("space", "sub"), None),
        P(("grp", "space", "sub"), None),
        P(),
        P("grp"),
        P(),
    )
    return jax.shard_map(
        local,
        mesh=mesh,
        in_specs=placed,
        out_specs=(
            P(("grp", "cuts"), None, ("space", "sub"), None),
            P(("grp", "cuts"), None, ("space", "sub"), None),
        ),
        check_vma=False,
    )
```

```python
import functools
import jax
import jax.numpy as jnp
from jax import lax
from jax.experimental import pallas as pl
from jax.experimental.pallas import tpu as pltpu
from jax.sharding import PartitionSpec as P

JOULE_GAIN = 0.5
MESH = pl.DeviceIdType.MESH
F32 = jnp.float32
BF16 = jnp.bfloat16


def pieces(values):
    high = values.astype(BF16)
    low = (values - high.astype(F32)).astype(BF16)
    return jnp.concatenate([high, low], axis=1)


def advance(sums, turn_amps, keep, mix):
    change = sums[0][1] + turn_amps
    magnet = sums[0][0] + change
    thermal = sums[1][0] + sums[1][1] + JOULE_GAIN * change * change
    return keep * magnet + mix * thermal, mix * magnet + keep * thermal


def link_factors(coupling, span):
    coupled = span * coupling
    diagonal = 1.0 + coupled
    offdiag = 0.5 * coupled
    determinant = diagonal * diagonal - offdiag * offdiag
    return diagonal / determinant, offdiag / determinant


def kernel(
    sizes, starts_hbm, prev_hbm, zone_hbm, mat_hbm, current_hbm, bounds_hbm,
    ends_ref, new_ref, pbuf, spread_ref,
    mat_ref, current_ref, bounds_ref, prev_ref, zone_ref, gather_ref, s0, s1, rf, fl, wt, pqs, zt, zb, mu, md, ht, hb, cf, grid_c, tbuf, ybuf,
    in_sem, send_near, recv_near, send_c, recv_c,
):
    cuts, nsub, tiles, lc, rows, cols, zones, half = sizes
    crow, ccol = rows // 4, cols // 4
    chunks = rows // 8
    cut = lax.axis_index("cuts")
    tile = lax.axis_index("space") * nsub + lax.axis_index("sub")
    has_up = tile > 0
    has_down = tile < tiles - 1
    base = cut * lc

    def where_is(side, cut_no=None):
        other = tile + (side - 1)
        place = {"space": lax.div(other, nsub), "sub": lax.rem(other, nsub)}
        if cut_no is not None:
            place["cuts"] = cut_no
        return place

    def on_side(side):
        if side == 1:
            return lambda fn: fn()
        return pl.when(has_up if side == 0 else has_down)

    load_zone = pltpu.make_async_copy(zone_hbm, zone_ref, in_sem.at[1])
    load_zone.start()
    small = [
        pltpu.make_async_copy(source, target, in_sem.at[3 + k])
        for k, (source, target) in enumerate(
            ((mat_hbm, mat_ref), (current_hbm, current_ref), (bounds_hbm, bounds_ref))
        )
    ]
    for copy in small:
        copy.start()
    load = pltpu.make_async_copy(starts_hbm, s0.at[:, :, pl.ds(8, rows), :], in_sem.at[0])
    load.start()
    load_prev = pltpu.make_async_copy(prev_hbm, prev_ref, in_sem.at[2])
    load_prev.start()

    barrier = pltpu.get_barrier_semaphore()
    for side in (0, 2):
        @on_side(side)
        def _():
            pl.semaphore_signal(barrier, inc=1, device_id=where_is(side), device_id_type=MESH)
    for step in range(1, cuts):
        other_cut = lax.rem(cut + step, cuts)
        for side in range(3):
            @on_side(side)
            def _():
                pl.semaphore_signal(
                    barrier, inc=1, device_id=where_is(side, other_cut), device_id_type=MESH
                )

    row8 = lax.broadcasted_iota(jnp.int32, (8, cols), 0)
    col8 = lax.broadcasted_iota(jnp.int32, (8, cols), 1)
    rowh = lax.broadcasted_iota(jnp.int32, (2 * half, cols), 0)
    colh = lax.broadcasted_iota(jnp.int32, (2 * half, cols), 1)

    def lookup(zone):
        found = [jnp.full(zone.shape, mat_ref[m, 0], F32) for m in range(4)]
        for zone_no in range(1, zones):
            present = zone == zone_no
            found = [jnp.where(present, mat_ref[m, zone_no], found[m]) for m in range(4)]
        return found

    def restricted(values, buf):
        count = values.shape[0]
        buf[0:count, :] = jnp.dot(
            pieces(values), gather_ref[...], preferred_element_type=F32
        )
        total = buf[pl.ds(0, count // 4, stride=4), :]
        for part in range(1, 4):
            total = total + buf[pl.ds(part, count // 4, stride=4), :]
        return total

    tall_row = lax.broadcasted_iota(jnp.int32, (cols, ccol), 0)
    tall_col = lax.broadcasted_iota(jnp.int32, (cols, ccol), 1)
    wide_row = lax.broadcasted_iota(jnp.int32, (ccol, cols), 0)
    wide_col = lax.broadcasted_iota(jnp.int32, (ccol, cols), 1)
    gather = jnp.where((tall_row >> 2) == tall_col, 0.0625, 0.0).astype(BF16)
    spread = jnp.where((wide_col >> 2) == wide_row, 1.0, 0.0).astype(BF16)
    for part in range(2):
        gather_ref[part * cols : (part + 1) * cols, :] = gather
        spread_ref[part * ccol : (part + 1) * ccol, :] = spread

    for copy in small:
        copy.wait()
    load_zone.wait()
    for i in range(chunks):
        found = lookup(zone_ref[8 * i : 8 * i + 8, :])
        for m in range(4):
            fl[m, 8 * i : 8 * i + 8, :] = found[m]
        for m in range(2):
            rf[m, 8 + 8 * i : 16 + 8 * i, :] = found[m]
        keep, mix = link_factors(found[2], 1.0)
        pqs[0, 8 * i : 8 * i + 8, :] = keep
        pqs[1, 8 * i : 8 * i + 8, :] = mix
        pqs[2, 8 * i : 8 * i + 8, :] = found[3]

    load.wait()
    if lc < half:
        mu[...] = jnp.zeros(mu.shape, F32)
        md[...] = jnp.zeros(md.shape, F32)
    for n in range(lc):
        for m in range(2):
            mu[m, half + n : half + n + 1, :] = s0[n, m, 8:9, :]
            mu[m, n : n + 1, :] = s0[n, m, 9:10, :]
            md[m, n : n + 1, :] = s0[n, m, rows + 7 : rows + 8, :]
            md[m, half + n : half + n + 1, :] = s0[n, m, rows + 6 : rows + 7, :]

    def lateral(value, edge, col):
        width = value.shape[1]
        left = jnp.where(col == 0, edge, pltpu.roll(value, 1, 1))
        right = jnp.where(col == width - 1, edge, pltpu.roll(value, width - 1, 1))
        return 0.5 * (value + left), 0.5 * (value + right)

    def five(center, up, down, edge, col):
        west, east = lateral(center, edge, col)
        north = 0.5 * (center + up)
        south = 0.5 * (center + down)
        width = center.shape[1]
        return (
            jnp.where(col == width - 1, 0.0, east),
            jnp.where(col == 0, 0.0, west),
            north,
            south,
            (west + east) + (north + south),
        )

    def make_weights(i):
        low = 8 + 8 * i
        for m in range(2):
            made = five(
                rf[m, low : low + 8, :], rf[m, low - 1 : low + 7, :],
                rf[m, low + 1 : low + 9, :], mat_ref[m, 0], col8,
            )
            for k in range(5):
                wt[m, k, 8 * i : 8 * i + 8, :] = made[k]

    def spread_sum(weights, center, up, down):
        width = center.shape[1]
        east, west, north, south, whole = weights
        total = east * pltpu.roll(center, width - 1, 1) + west * pltpu.roll(center, 1, 1)
        return (total + (north * up + south * down)) - whole * center

    def amps_at(slice_no, offset):
        return current_ref[bounds_ref[slice_no] + offset].astype(F32) * 0.001

    amps = [[amps_at(base + n, j) for j in range(2)] for n in range(lc)]

    def fine_chunk(source, n, i, amperes):
        low = 8 + 8 * i
        at = slice(8 * i, 8 * i + 8)
        sums = []
        for m in range(2):
            center = source[n, m, low : low + 8, :]
            weights = [wt[m, k, at, :] for k in range(5)]
            sums.append((center, spread_sum(
                weights, center, source[n, m, low - 1 : low + 7, :],
                source[n, m, low + 1 : low + 9, :],
            )))
        return advance(sums, pqs[2, at, :] * amperes, pqs[0, at, :], pqs[1, at, :])

    def first_step(n, i):
        out = fine_chunk(s0, n, i, amps_at(base + n, 0))
        for m in range(2):
            s1[n, m, 8 + 8 * i : 16 + 8 * i, :] = out[m]

    for i in range(1, chunks - 1):
        make_weights(i)
    @pl.loop(0, lc)
    def _(n):
        for i in range(1, chunks - 1):
            first_step(n, i)

    own_c = restricted(fl[...].reshape(4 * rows, cols), tbuf)
    for m in range(4):
        cf[m, crow : 2 * crow, :] = own_c[m * crow : (m + 1) * crow]
    ups = jnp.where(has_up, 1, 0) + jnp.where(has_down, 1, 0)
    pl.semaphore_wait(barrier, ups + (cuts - 1) * (1 + ups))

    def near(what, side):
        if what == 0:
            source = zone_ref.at[0:8] if side == 0 else zone_ref.at[rows - 8 : rows]
            target = zb if side == 0 else zt
        elif what == 1:
            source = mu if side == 0 else md
            target = hb if side == 0 else ht
        else:
            source = cf.at[:, pl.ds(crow, crow), :]
            target = cf.at[:, pl.ds(2 * crow if side == 0 else 0, crow), :]
        return pltpu.make_async_remote_copy(
            src_ref=source,
            dst_ref=target,
            send_sem=send_near.at[what, side // 2],
            recv_sem=recv_near.at[what, side // 2],
            device_id=where_is(side),
            device_id_type=MESH,
        )

    def coarse_copy(side, first, count, mark, kind, dest):
        return pltpu.make_async_remote_copy(
            src_ref=grid_c.at[pl.ds(first, count), :, pl.ds(crow, crow), :],
            dst_ref=grid_c.at[pl.ds(first, count), :, pl.ds((2 - side) * crow, crow), :],
            send_sem=send_c.at[dest, side, kind],
            recv_sem=recv_c.at[2 - side, mark],
            device_id=where_is(side, None if dest == 0 else dest),
            device_id_type=MESH,
        )

    def each_coarse_send(first, count, mark, kind, action):
        for side in (0, 2):
            @on_side(side)
            def _():
                action(coarse_copy(side, first, count, mark, kind, 0))
        for dest in range(1, cuts):
            @pl.when(cut < dest)
            def _():
                for side in (1, 0, 2):
                    @on_side(side)
                    def _():
                        action(coarse_copy(side, first, count, mark, kind, dest))

    def await_coarse(side, first, count, mark):
        pltpu.make_async_remote_copy(
            src_ref=grid_c.at[pl.ds(first, count), :, pl.ds(crow, crow), :],
            dst_ref=grid_c.at[pl.ds(first, count), :, pl.ds(side * crow, crow), :],
            send_sem=send_c.at[0, 0, 0],
            recv_sem=recv_c.at[side, mark],
            device_id=where_is(1, lax.rem(cut + 1, cuts)),
            device_id_type=MESH,
        ).wait_recv()

    for what in (0, 1):
        for side in (0, 2):
            @on_side(side)
            def _():
                near(what, side).start()

    @pl.when(jnp.logical_not(has_up))
    def _():
        zt[...] = jnp.zeros(zt.shape, jnp.int32)
        ht[...] = jnp.zeros(ht.shape, F32)
        for m in range(4):
            cf[m, 0:crow, :] = jnp.full((crow, ccol), mat_ref[m, 0], F32)
        grid_c[:, :, 0:crow, :] = jnp.zeros(grid_c.shape[:2] + (crow, ccol), F32)

    @pl.when(jnp.logical_not(has_down))
    def _():
        zb[...] = jnp.zeros(zb.shape, jnp.int32)
        hb[...] = jnp.zeros(hb.shape, F32)
        for m in range(4):
            cf[m, 2 * crow : 3 * crow, :] = jnp.full((crow, ccol), mat_ref[m, 0], F32)
        grid_c[:, :, 2 * crow : 3 * crow, :] = jnp.zeros(grid_c.shape[:2] + (crow, ccol), F32)

    for side in (0, 2):
        @on_side(side)
        def _():
            near(2, side).start()

    @pl.when(cut == 0)
    def _():
        first = restricted(s0[0, :, 8 : 8 + rows, :].reshape(2 * rows, cols), tbuf)
        for m in range(2):
            grid_c[0, m, crow : 2 * crow, :] = first[m * crow : (m + 1) * crow]
        each_coarse_send(0, 1, 0, 0, lambda copy: copy.start())

    for side in (0, 2):
        @on_side(side)
        def _():
            near(0, 2 - side).wait_recv()
    above = lookup(zt[...])
    below = lookup(zb[...])
    for m in range(2):
        rf[m, 0:8, :] = above[m]
        rf[m, rows + 8 : rows + 16, :] = below[m]

    for i in (0, chunks - 1):
        make_weights(i)

    def both(top, bottom):
        shape = (2 * half, cols)
        return jnp.where(rowh < half, jnp.broadcast_to(top, shape), jnp.broadcast_to(bottom, shape))

    edge_weights = []
    for m in range(2):
        center = both(rf[m, 7:8, :], rf[m, rows + 8 : rows + 9, :])
        outer = both(rf[m, 6:7, :], rf[m, rows + 9 : rows + 10, :])
        inner = both(rf[m, 8:9, :], rf[m, rows + 7 : rows + 8, :])
        edge_weights.append(five(center, outer, inner, mat_ref[m, 0], colh))
    edge_keep, edge_mix = link_factors(both(above[2][7:8], below[2][0:1]), 1.0)
    edge_amps = jnp.zeros((2 * half, cols), F32)
    for n in range(lc):
        edge_amps = jnp.where(
            jnp.logical_or(rowh == n, rowh == half + n), amps[n][0], edge_amps
        )
    edge_turn = both(above[3][7:8], below[3][0:1]) * edge_amps

    for side in (0, 2):
        @on_side(side)
        def _():
            near(1, 2 - side).wait_recv()

    edge_sums = []
    for m in range(2):
        center = jnp.where(rowh < half, ht[m], hb[m])
        outer = pltpu.roll(jnp.where(rowh < half, hb[m], ht[m]), half, 0)
        inner = pltpu.roll(jnp.where(rowh < half, md[m], mu[m]), half, 0)
        edge_sums.append((center, spread_sum(edge_weights[m], center, outer, inner)))
        for n in range(lc):
            s0[n, m, 7:8, :] = ht[m, n : n + 1, :]
            s0[n, m, rows + 8 : rows + 9, :] = hb[m, half + n : half + n + 1, :]
    edge_out = advance(edge_sums, edge_turn, edge_keep, edge_mix)
    inside = jnp.where(
        rowh < half, jnp.where(has_up, 1, 0), jnp.where(has_down, 1, 0)
    ) > 0
    for m in range(2):
        kept = jnp.where(inside, edge_out[m], 0.0)
        for n in range(lc):
            s1[n, m, 7:8, :] = kept[n : n + 1]
            s1[n, m, rows + 8 : rows + 9, :] = kept[half + n : half + n + 1]

    load_prev.wait()
    @pl.loop(0, lc)
    def _(n):
        for i in (0, chunks - 1):
            first_step(n, i)
        for i in range(chunks):
            out = fine_chunk(s1, n, i, amps_at(base + n, 1))
            for m in range(2):
                ends_ref[n, m, 8 * i : 8 * i + 8, :] = out[m]
        mean = restricted(ends_ref[n].reshape(2 * rows, cols), tbuf)
        for m in range(2):
            grid_c[base + n + 1, m, crow : 2 * crow, :] = (
                mean[m * crow : (m + 1) * crow] - prev_ref[n, m]
            )
    each_coarse_send(base + 1, lc, cut + 1, 1, lambda copy: copy.start())

    for side in (0, 2):
        @on_side(side)
        def _():
            near(2, 2 - side).wait_recv()
    tall = 3 * crow
    crows = lax.broadcasted_iota(jnp.int32, (tall, ccol), 0)
    ccols = lax.broadcasted_iota(jnp.int32, (tall, ccol), 1)
    in_grid = jnp.logical_and(
        jnp.where(crows < crow, jnp.where(has_up, 1, 0), 1) > 0,
        jnp.where(crows >= 2 * crow, jnp.where(has_down, 1, 0), 1) > 0,
    )
    coarse_weights = []
    for m in range(2):
        center = cf[m] * 0.125
        coarse_weights.append(five(
            center, pltpu.roll(center, 1, 0), pltpu.roll(center, tall - 1, 0),
            mat_ref[m, 0] * 0.125, ccols,
        ))
    coarse_keep, coarse_mix = link_factors(cf[2], 2.0)
    coarse_turn = 2.0 * cf[3]

    def coarse_step(state, amperes):
        sums = []
        for m in range(2):
            center = state[m]
            sums.append((center, spread_sum(
                coarse_weights[m], center, pltpu.roll(center, 1, 0),
                pltpu.roll(center, tall - 1, 0),
            )))
        return advance(sums, coarse_turn * amperes, coarse_keep, coarse_mix)

    def following(out, g):
        return [jnp.where(in_grid, out[m] + grid_c[g, m], 0.0) for m in range(2)]

    @pl.when(cut > 0)
    def _():
        await_coarse(1, 0, 1, 0)
    for side in (0, 2):
        @on_side(side)
        def _():
            await_coarse(side, 0, 1, 0)
    for m in range(2):
        ybuf[m] = grid_c[0, m]
    for before in range(cuts - 1):
        @pl.when(cut > before)
        def _():
            for side in range(3):
                @on_side(side)
                def _():
                    await_coarse(side, before * lc + 1, lc, before + 1)
            state = [ybuf[m] for m in range(2)]
            for n in range(lc):
                slice_no = before * lc + n
                out = coarse_step(state, amps_at(slice_no, 0))
                state = following(out, slice_no + 1)
            for m in range(2):
                ybuf[m] = state[m]

    for side in (0, 2):
        @on_side(side)
        def _():
            await_coarse(side, base + 1, lc, cut + 1)
    state = [ybuf[m] for m in range(2)]
    for n in range(lc):
        out = coarse_step(state, amps[n][0])
        for m in range(2):
            fresh = out[m][crow : 2 * crow]
            new_ref[n, m] = fresh
            gain = fresh - prev_ref[n, m]
            for part in range(4):
                pbuf[n, pl.ds(m * rows + part, crow, stride=4), :] = gain
        if n < lc - 1:
            state = following(out, base + n + 1)

    for what in range(3):
        for side in (0, 2):
            @on_side(side)
            def _():
                near(what, side).wait_send()

    @pl.when(cut == 0)
    def _():
        each_coarse_send(0, 1, 0, 0, lambda copy: copy.wait_send())
    each_coarse_send(base + 1, lc, cut + 1, 1, lambda copy: copy.wait_send())


def finish(fine_ref, new_ref, pbuf, spread_ref, ends_out, new_out, total, sems):
    lc, _, rows, cols = fine_ref.shape
    copies = [pltpu.make_async_copy(new_ref, new_out, sems.at[lc])]
    copies[0].start()
    for n in range(lc):
        added = jnp.dot(pieces(pbuf[n]), spread_ref[...], preferred_element_type=F32)
        total[n] = fine_ref[n] + added.reshape(2, rows, cols)
        copies.append(pltpu.make_async_copy(total.at[n], ends_out.at[n], sems.at[n]))
        copies[-1].start()
    for copy in copies:
        copy.wait()


def solution(mesh):
    cuts, nsub = mesh.shape["cuts"], mesh.shape["sub"]
    tiles = mesh.shape["space"] * nsub

    def local(starts, coarse_prev, zone_ids, materials, current, bounds):
        lc, _, rows, cols = starts.shape
        crow, ccol = rows // 4, cols // 4
        half = max(4, lc)
        slices = lc * cuts
        sizes = (cuts, nsub, tiles, lc, rows, cols, materials.shape[1], half)
        vmem = pl.BlockSpec(memory_space=pltpu.VMEM)
        hbm = pl.BlockSpec(memory_space=pltpu.HBM)
        fine, new, risen, spread = pl.pallas_call(
            functools.partial(kernel, sizes),
            out_shape=(
                jax.ShapeDtypeStruct(starts.shape, F32),
                jax.ShapeDtypeStruct(coarse_prev.shape, F32),
                jax.ShapeDtypeStruct((lc, 2 * rows, ccol), F32),
                jax.ShapeDtypeStruct((2 * ccol, cols), BF16),
            ),
            in_specs=[hbm] * 6,
            out_specs=(vmem,) * 4,
            scratch_shapes=[
                pltpu.SMEM(materials.shape, F32),
                pltpu.SMEM(current.shape, jnp.int32),
                pltpu.SMEM(bounds.shape, jnp.int32),
                pltpu.VMEM((lc, 2, crow, ccol), F32),
                pltpu.VMEM((rows, cols), jnp.int32),
                pltpu.VMEM((2 * cols, ccol), BF16),
                pltpu.VMEM((lc, 2, rows + 16, cols), F32),
                pltpu.VMEM((lc, 2, rows + 16, cols), F32),
                pltpu.VMEM((2, rows + 16, cols), F32),
                pltpu.VMEM((4, rows, cols), F32),
                pltpu.VMEM((2, 5, rows, cols), F32),
                pltpu.VMEM((3, rows, cols), F32),
                pltpu.VMEM((8, cols), jnp.int32),
                pltpu.VMEM((8, cols), jnp.int32),
                pltpu.VMEM((2, 2 * half, cols), F32),
                pltpu.VMEM((2, 2 * half, cols), F32),
                pltpu.VMEM((2, 2 * half, cols), F32),
                pltpu.VMEM((2, 2 * half, cols), F32),
                pltpu.VMEM((4, 3 * crow, ccol), F32),
                pltpu.VMEM((slices + 1, 2, 3 * crow, ccol), F32),
                pltpu.VMEM((4 * rows, ccol), F32),
                pltpu.VMEM((2, 3 * crow, ccol), F32),
                pltpu.SemaphoreType.DMA((6,)),
                pltpu.SemaphoreType.DMA((3, 2)),
                pltpu.SemaphoreType.DMA((3, 2)),
                pltpu.SemaphoreType.DMA((cuts, 3, 2)),
                pltpu.SemaphoreType.DMA((3, cuts + 1)),
            ],
            compiler_params=pltpu.CompilerParams(
                collective_id=0, has_side_effects=True, vmem_limit_bytes=32 * 1024 * 1024
            ),
        )(*(
            pltpu.with_memory_space_constraint(given, pltpu.HBM)
            for given in (starts, coarse_prev, zone_ids, materials, current, bounds)
        ))
        return pl.pallas_call(
            finish,
            out_shape=(
                jax.ShapeDtypeStruct(starts.shape, F32),
                jax.ShapeDtypeStruct(coarse_prev.shape, F32),
            ),
            in_specs=[vmem] * 4,
            out_specs=(hbm, hbm),
            scratch_shapes=[
                pltpu.VMEM(starts.shape, F32),
                pltpu.SemaphoreType.DMA((lc + 1,)),
            ],
            compiler_params=pltpu.CompilerParams(vmem_limit_bytes=16 * 1024 * 1024),
        )(fine, new, risen, spread)

    placed = (
        P(("grp", "cuts"), None, ("space", "sub"), None),
        P(("grp", "cuts"), None, ("space", "sub"), None),
        P(("grp", "space", "sub"), None),
        P(),
        P("grp"),
        P(),
    )
    return jax.shard_map(
        local,
        mesh=mesh,
        in_specs=placed,
        out_specs=(
            P(("grp", "cuts"), None, ("space", "sub"), None),
            P(("grp", "cuts"), None, ("space", "sub"), None),
        ),
        check_vma=False,
    )
```

```python
import functools
import jax
import jax.numpy as jnp
from jax import lax
from jax.experimental import pallas as pl
from jax.experimental.pallas import tpu as pltpu
from jax.sharding import PartitionSpec as P

JOULE_GAIN = 0.5
MESH = pl.DeviceIdType.MESH
F32 = jnp.float32
BF16 = jnp.bfloat16


def pieces(values):
    high = values.astype(BF16)
    low = (values - high.astype(F32)).astype(BF16)
    return jnp.concatenate([high, low], axis=1)


def advance(sums, turn_amps, keep, mix):
    change = sums[0][1] + turn_amps
    magnet = sums[0][0] + change
    thermal = sums[1][0] + sums[1][1] + JOULE_GAIN * change * change
    return keep * magnet + mix * thermal, mix * magnet + keep * thermal


def link_factors(coupling, span):
    coupled = span * coupling
    diagonal = 1.0 + coupled
    offdiag = 0.5 * coupled
    determinant = diagonal * diagonal - offdiag * offdiag
    return diagonal / determinant, offdiag / determinant


def kernel(
    sizes, starts_hbm, prev_hbm, zone_hbm, mat_hbm, current_hbm, bounds_hbm,
    ends_ref, new_ref, pbuf, spread_ref,
    mat_ref, current_ref, bounds_ref, prev_ref, zone_ref, gather_ref, s0, s1, rf, fl, wt, pqs, zt, zb, mu, md, ht, hb, cf, grid_c, tbuf, ybuf,
    in_sem, send_near, recv_near, send_c, recv_c,
):
    cuts, nsub, tiles, lc, rows, cols, zones, half = sizes
    crow, ccol = rows // 4, cols // 4
    chunks = rows // 8
    cut = lax.axis_index("cuts")
    tile = lax.axis_index("space") * nsub + lax.axis_index("sub")
    has_up = tile > 0
    has_down = tile < tiles - 1
    base = cut * lc

    def where_is(side, cut_no=None):
        other = tile + (side - 1)
        place = {"space": lax.div(other, nsub), "sub": lax.rem(other, nsub)}
        if cut_no is not None:
            place["cuts"] = cut_no
        return place

    def on_side(side):
        if side == 1:
            return lambda fn: fn()
        return pl.when(has_up if side == 0 else has_down)

    load_zone = pltpu.make_async_copy(zone_hbm, zone_ref, in_sem.at[1])
    load_zone.start()
    small = [
        pltpu.make_async_copy(source, target, in_sem.at[3 + k])
        for k, (source, target) in enumerate(
            ((mat_hbm, mat_ref), (current_hbm, current_ref), (bounds_hbm, bounds_ref))
        )
    ]
    for copy in small:
        copy.start()
    load = pltpu.make_async_copy(starts_hbm, s0.at[:, :, pl.ds(8, rows), :], in_sem.at[0])
    load.start()
    load_prev = pltpu.make_async_copy(prev_hbm, prev_ref, in_sem.at[2])
    load_prev.start()

    barrier = pltpu.get_barrier_semaphore()
    for side in (0, 2):
        @on_side(side)
        def _():
            pl.semaphore_signal(barrier, inc=1, device_id=where_is(side), device_id_type=MESH)
    for step in range(1, cuts):
        other_cut = lax.rem(cut + step, cuts)
        for side in range(3):
            @on_side(side)
            def _():
                pl.semaphore_signal(
                    barrier, inc=1, device_id=where_is(side, other_cut), device_id_type=MESH
                )

    row8 = lax.broadcasted_iota(jnp.int32, (8, cols), 0)
    col8 = lax.broadcasted_iota(jnp.int32, (8, cols), 1)
    rowh = lax.broadcasted_iota(jnp.int32, (2 * half, cols), 0)
    colh = lax.broadcasted_iota(jnp.int32, (2 * half, cols), 1)

    def lookup(zone):
        found = [jnp.full(zone.shape, mat_ref[m, 0], F32) for m in range(4)]
        for zone_no in range(1, zones):
            present = zone == zone_no
            found = [jnp.where(present, mat_ref[m, zone_no], found[m]) for m in range(4)]
        return found

    def restricted(values, buf):
        count = values.shape[0]
        buf[0:count, :] = jnp.dot(
            pieces(values), gather_ref[...], preferred_element_type=F32
        )
        total = buf[pl.ds(0, count // 4, stride=4), :]
        for part in range(1, 4):
            total = total + buf[pl.ds(part, count // 4, stride=4), :]
        return total

    tall_row = lax.broadcasted_iota(jnp.int32, (cols, ccol), 0)
    tall_col = lax.broadcasted_iota(jnp.int32, (cols, ccol), 1)
    wide_row = lax.broadcasted_iota(jnp.int32, (ccol, cols), 0)
    wide_col = lax.broadcasted_iota(jnp.int32, (ccol, cols), 1)
    gather = jnp.where((tall_row >> 2) == tall_col, 0.0625, 0.0).astype(BF16)
    spread = jnp.where((wide_col >> 2) == wide_row, 1.0, 0.0).astype(BF16)
    for part in range(2):
        gather_ref[part * cols : (part + 1) * cols, :] = gather
        spread_ref[part * ccol : (part + 1) * ccol, :] = spread

    for copy in small:
        copy.wait()
    load_zone.wait()
    for i in range(chunks):
        found = lookup(zone_ref[8 * i : 8 * i + 8, :])
        for m in range(4):
            fl[m, 8 * i : 8 * i + 8, :] = found[m]
        for m in range(2):
            rf[m, 8 + 8 * i : 16 + 8 * i, :] = found[m]
        keep, mix = link_factors(found[2], 1.0)
        pqs[0, 8 * i : 8 * i + 8, :] = keep
        pqs[1, 8 * i : 8 * i + 8, :] = mix
        pqs[2, 8 * i : 8 * i + 8, :] = found[3]

    load.wait()
    if lc < half:
        mu[...] = jnp.zeros(mu.shape, F32)
        md[...] = jnp.zeros(md.shape, F32)
    for n in range(lc):
        for m in range(2):
            mu[m, half + n : half + n + 1, :] = s0[n, m, 8:9, :]
            mu[m, n : n + 1, :] = s0[n, m, 9:10, :]
            md[m, n : n + 1, :] = s0[n, m, rows + 7 : rows + 8, :]
            md[m, half + n : half + n + 1, :] = s0[n, m, rows + 6 : rows + 7, :]

    ups = jnp.where(has_up, 1, 0) + jnp.where(has_down, 1, 0)
    pl.semaphore_wait(barrier, ups + (cuts - 1) * (1 + ups))

    def near(what, side):
        if what == 0:
            source = zone_ref.at[0:8] if side == 0 else zone_ref.at[rows - 8 : rows]
            target = zb if side == 0 else zt
        elif what == 1:
            source = mu if side == 0 else md
            target = hb if side == 0 else ht
        else:
            source = cf.at[:, pl.ds(crow, crow), :]
            target = cf.at[:, pl.ds(2 * crow if side == 0 else 0, crow), :]
        return pltpu.make_async_remote_copy(
            src_ref=source,
            dst_ref=target,
            send_sem=send_near.at[what, side // 2],
            recv_sem=recv_near.at[what, side // 2],
            device_id=where_is(side),
            device_id_type=MESH,
        )

    def coarse_copy(side, first, count, mark, kind, dest):
        return pltpu.make_async_remote_copy(
            src_ref=grid_c.at[pl.ds(first, count), :, pl.ds(crow, crow), :],
            dst_ref=grid_c.at[pl.ds(first, count), :, pl.ds((2 - side) * crow, crow), :],
            send_sem=send_c.at[dest, side, kind],
            recv_sem=recv_c.at[2 - side, mark],
            device_id=where_is(side, None if dest == 0 else dest),
            device_id_type=MESH,
        )

    def each_coarse_send(first, count, mark, kind, action):
        for side in (0, 2):
            @on_side(side)
            def _():
                action(coarse_copy(side, first, count, mark, kind, 0))
        for dest in range(1, cuts):
            @pl.when(cut < dest)
            def _():
                for side in (1, 0, 2):
                    @on_side(side)
                    def _():
                        action(coarse_copy(side, first, count, mark, kind, dest))

    def await_coarse(side, first, count, mark):
        pltpu.make_async_remote_copy(
            src_ref=grid_c.at[pl.ds(first, count), :, pl.ds(crow, crow), :],
            dst_ref=grid_c.at[pl.ds(first, count), :, pl.ds(side * crow, crow), :],
            send_sem=send_c.at[0, 0, 0],
            recv_sem=recv_c.at[side, mark],
            device_id=where_is(1, lax.rem(cut + 1, cuts)),
            device_id_type=MESH,
        ).wait_recv()

    for what in (0, 1):
        for side in (0, 2):
            @on_side(side)
            def _():
                near(what, side).start()

    @pl.when(jnp.logical_not(has_up))
    def _():
        zt[...] = jnp.zeros(zt.shape, jnp.int32)
        ht[...] = jnp.zeros(ht.shape, F32)
        for m in range(4):
            cf[m, 0:crow, :] = jnp.full((crow, ccol), mat_ref[m, 0], F32)
        grid_c[:, :, 0:crow, :] = jnp.zeros(grid_c.shape[:2] + (crow, ccol), F32)

    @pl.when(jnp.logical_not(has_down))
    def _():
        zb[...] = jnp.zeros(zb.shape, jnp.int32)
        hb[...] = jnp.zeros(hb.shape, F32)
        for m in range(4):
            cf[m, 2 * crow : 3 * crow, :] = jnp.full((crow, ccol), mat_ref[m, 0], F32)
        grid_c[:, :, 2 * crow : 3 * crow, :] = jnp.zeros(grid_c.shape[:2] + (crow, ccol), F32)

    own_c = restricted(fl[...].reshape(4 * rows, cols), tbuf)
    for m in range(4):
        cf[m, crow : 2 * crow, :] = own_c[m * crow : (m + 1) * crow]
    for side in (0, 2):
        @on_side(side)
        def _():
            near(2, side).start()

    @pl.when(cut == 0)
    def _():
        first = restricted(s0[0, :, 8 : 8 + rows, :].reshape(2 * rows, cols), tbuf)
        for m in range(2):
            grid_c[0, m, crow : 2 * crow, :] = first[m * crow : (m + 1) * crow]
        each_coarse_send(0, 1, 0, 0, lambda copy: copy.start())

    def lateral(value, edge, col):
        width = value.shape[1]
        left = jnp.where(col == 0, edge, pltpu.roll(value, 1, 1))
        right = jnp.where(col == width - 1, edge, pltpu.roll(value, width - 1, 1))
        return 0.5 * (value + left), 0.5 * (value + right)

    def five(center, up, down, edge, col):
        west, east = lateral(center, edge, col)
        north = 0.5 * (center + up)
        south = 0.5 * (center + down)
        width = center.shape[1]
        return (
            jnp.where(col == width - 1, 0.0, east),
            jnp.where(col == 0, 0.0, west),
            north,
            south,
            (west + east) + (north + south),
        )

    def make_weights(i):
        low = 8 + 8 * i
        for m in range(2):
            made = five(
                rf[m, low : low + 8, :], rf[m, low - 1 : low + 7, :],
                rf[m, low + 1 : low + 9, :], mat_ref[m, 0], col8,
            )
            for k in range(5):
                wt[m, k, 8 * i : 8 * i + 8, :] = made[k]

    def spread_sum(weights, center, up, down):
        width = center.shape[1]
        east, west, north, south, whole = weights
        total = east * pltpu.roll(center, width - 1, 1) + west * pltpu.roll(center, 1, 1)
        return (total + (north * up + south * down)) - whole * center

    def amps_at(slice_no, offset):
        return current_ref[bounds_ref[slice_no] + offset].astype(F32) * 0.001

    amps = [[amps_at(base + n, j) for j in range(2)] for n in range(lc)]

    def fine_chunk(source, n, i, amperes):
        low = 8 + 8 * i
        at = slice(8 * i, 8 * i + 8)
        sums = []
        for m in range(2):
            center = source[n, m, low : low + 8, :]
            weights = [wt[m, k, at, :] for k in range(5)]
            sums.append((center, spread_sum(
                weights, center, source[n, m, low - 1 : low + 7, :],
                source[n, m, low + 1 : low + 9, :],
            )))
        return advance(sums, pqs[2, at, :] * amperes, pqs[0, at, :], pqs[1, at, :])

    def first_step(n, i):
        out = fine_chunk(s0, n, i, amps[n][0])
        for m in range(2):
            s1[n, m, 8 + 8 * i : 16 + 8 * i, :] = out[m]

    for i in range(1, chunks - 1):
        make_weights(i)
    for n in range(lc):
        for i in range(1, chunks - 1):
            first_step(n, i)

    for side in (0, 2):
        @on_side(side)
        def _():
            near(0, 2 - side).wait_recv()
    above = lookup(zt[...])
    below = lookup(zb[...])
    for m in range(2):
        rf[m, 0:8, :] = above[m]
        rf[m, rows + 8 : rows + 16, :] = below[m]

    for i in (0, chunks - 1):
        make_weights(i)

    def both(top, bottom):
        shape = (2 * half, cols)
        return jnp.where(rowh < half, jnp.broadcast_to(top, shape), jnp.broadcast_to(bottom, shape))

    edge_weights = []
    for m in range(2):
        center = both(rf[m, 7:8, :], rf[m, rows + 8 : rows + 9, :])
        outer = both(rf[m, 6:7, :], rf[m, rows + 9 : rows + 10, :])
        inner = both(rf[m, 8:9, :], rf[m, rows + 7 : rows + 8, :])
        edge_weights.append(five(center, outer, inner, mat_ref[m, 0], colh))
    edge_keep, edge_mix = link_factors(both(above[2][7:8], below[2][0:1]), 1.0)
    edge_amps = jnp.zeros((2 * half, cols), F32)
    for n in range(lc):
        edge_amps = jnp.where(
            jnp.logical_or(rowh == n, rowh == half + n), amps[n][0], edge_amps
        )
    edge_turn = both(above[3][7:8], below[3][0:1]) * edge_amps

    for side in (0, 2):
        @on_side(side)
        def _():
            near(1, 2 - side).wait_recv()

    edge_sums = []
    for m in range(2):
        center = jnp.where(rowh < half, ht[m], hb[m])
        outer = pltpu.roll(jnp.where(rowh < half, hb[m], ht[m]), half, 0)
        inner = pltpu.roll(jnp.where(rowh < half, md[m], mu[m]), half, 0)
        edge_sums.append((center, spread_sum(edge_weights[m], center, outer, inner)))
        for n in range(lc):
            s0[n, m, 7:8, :] = ht[m, n : n + 1, :]
            s0[n, m, rows + 8 : rows + 9, :] = hb[m, half + n : half + n + 1, :]
    edge_out = advance(edge_sums, edge_turn, edge_keep, edge_mix)
    inside = jnp.where(
        rowh < half, jnp.where(has_up, 1, 0), jnp.where(has_down, 1, 0)
    ) > 0
    for m in range(2):
        kept = jnp.where(inside, edge_out[m], 0.0)
        for n in range(lc):
            s1[n, m, 7:8, :] = kept[n : n + 1]
            s1[n, m, rows + 8 : rows + 9, :] = kept[half + n : half + n + 1]

    load_prev.wait()
    for n in range(lc):
        for i in (0, chunks - 1):
            first_step(n, i)
        for i in range(chunks):
            out = fine_chunk(s1, n, i, amps[n][1])
            for m in range(2):
                ends_ref[n, m, 8 * i : 8 * i + 8, :] = out[m]
        mean = restricted(ends_ref[n].reshape(2 * rows, cols), tbuf)
        for m in range(2):
            grid_c[base + n + 1, m, crow : 2 * crow, :] = (
                mean[m * crow : (m + 1) * crow] - prev_ref[n, m]
            )
    each_coarse_send(base + 1, lc, cut + 1, 1, lambda copy: copy.start())

    for side in (0, 2):
        @on_side(side)
        def _():
            near(2, 2 - side).wait_recv()
    tall = 3 * crow
    crows = lax.broadcasted_iota(jnp.int32, (tall, ccol), 0)
    ccols = lax.broadcasted_iota(jnp.int32, (tall, ccol), 1)
    in_grid = jnp.logical_and(
        jnp.where(crows < crow, jnp.where(has_up, 1, 0), 1) > 0,
        jnp.where(crows >= 2 * crow, jnp.where(has_down, 1, 0), 1) > 0,
    )
    coarse_weights = []
    for m in range(2):
        center = cf[m] * 0.125
        coarse_weights.append(five(
            center, pltpu.roll(center, 1, 0), pltpu.roll(center, tall - 1, 0),
            mat_ref[m, 0] * 0.125, ccols,
        ))
    coarse_keep, coarse_mix = link_factors(cf[2], 2.0)
    coarse_turn = 2.0 * cf[3]

    def coarse_step(state, amperes):
        sums = []
        for m in range(2):
            center = state[m]
            sums.append((center, spread_sum(
                coarse_weights[m], center, pltpu.roll(center, 1, 0),
                pltpu.roll(center, tall - 1, 0),
            )))
        return advance(sums, coarse_turn * amperes, coarse_keep, coarse_mix)

    def following(out, g):
        return [jnp.where(in_grid, out[m] + grid_c[g, m], 0.0) for m in range(2)]

    @pl.when(cut > 0)
    def _():
        await_coarse(1, 0, 1, 0)
    for side in (0, 2):
        @on_side(side)
        def _():
            await_coarse(side, 0, 1, 0)
    for m in range(2):
        ybuf[m] = grid_c[0, m]
    for before in range(cuts - 1):
        @pl.when(cut > before)
        def _():
            for side in range(3):
                @on_side(side)
                def _():
                    await_coarse(side, before * lc + 1, lc, before + 1)
            state = [ybuf[m] for m in range(2)]
            for n in range(lc):
                slice_no = before * lc + n
                out = coarse_step(state, amps_at(slice_no, 0))
                state = following(out, slice_no + 1)
            for m in range(2):
                ybuf[m] = state[m]

    for side in (0, 2):
        @on_side(side)
        def _():
            await_coarse(side, base + 1, lc, cut + 1)
    state = [ybuf[m] for m in range(2)]
    for n in range(lc):
        out = coarse_step(state, amps[n][0])
        for m in range(2):
            fresh = out[m][crow : 2 * crow]
            new_ref[n, m] = fresh
            gain = fresh - prev_ref[n, m]
            for part in range(4):
                pbuf[n, pl.ds(m * rows + part, crow, stride=4), :] = gain
        if n < lc - 1:
            state = following(out, base + n + 1)

    for what in range(3):
        for side in (0, 2):
            @on_side(side)
            def _():
                near(what, side).wait_send()

    @pl.when(cut == 0)
    def _():
        each_coarse_send(0, 1, 0, 0, lambda copy: copy.wait_send())
    each_coarse_send(base + 1, lc, cut + 1, 1, lambda copy: copy.wait_send())


def finish(fine_ref, new_ref, pbuf, spread_ref, ends_out, new_out, total, sems):
    lc, _, rows, cols = fine_ref.shape
    copies = [pltpu.make_async_copy(new_ref, new_out, sems.at[lc])]
    copies[0].start()
    for n in range(lc):
        added = jnp.dot(pieces(pbuf[n]), spread_ref[...], preferred_element_type=F32)
        total[n] = fine_ref[n] + added.reshape(2, rows, cols)
        copies.append(pltpu.make_async_copy(total.at[n], ends_out.at[n], sems.at[n]))
        copies[-1].start()
    for copy in copies:
        copy.wait()


def solution(mesh):
    cuts, nsub = mesh.shape["cuts"], mesh.shape["sub"]
    tiles = mesh.shape["space"] * nsub

    def local(starts, coarse_prev, zone_ids, materials, current, bounds):
        lc, _, rows, cols = starts.shape
        crow, ccol = rows // 4, cols // 4
        half = max(4, lc)
        slices = lc * cuts
        sizes = (cuts, nsub, tiles, lc, rows, cols, materials.shape[1], half)
        vmem = pl.BlockSpec(memory_space=pltpu.VMEM)
        hbm = pl.BlockSpec(memory_space=pltpu.HBM)
        fine, new, risen, spread = pl.pallas_call(
            functools.partial(kernel, sizes),
            out_shape=(
                jax.ShapeDtypeStruct(starts.shape, F32),
                jax.ShapeDtypeStruct(coarse_prev.shape, F32),
                jax.ShapeDtypeStruct((lc, 2 * rows, ccol), F32),
                jax.ShapeDtypeStruct((2 * ccol, cols), BF16),
            ),
            in_specs=[hbm] * 6,
            out_specs=(vmem,) * 4,
            scratch_shapes=[
                pltpu.SMEM(materials.shape, F32),
                pltpu.SMEM(current.shape, jnp.int32),
                pltpu.SMEM(bounds.shape, jnp.int32),
                pltpu.VMEM((lc, 2, crow, ccol), F32),
                pltpu.VMEM((rows, cols), jnp.int32),
                pltpu.VMEM((2 * cols, ccol), BF16),
                pltpu.VMEM((lc, 2, rows + 16, cols), F32),
                pltpu.VMEM((lc, 2, rows + 16, cols), F32),
                pltpu.VMEM((2, rows + 16, cols), F32),
                pltpu.VMEM((4, rows, cols), F32),
                pltpu.VMEM((2, 5, rows, cols), F32),
                pltpu.VMEM((3, rows, cols), F32),
                pltpu.VMEM((8, cols), jnp.int32),
                pltpu.VMEM((8, cols), jnp.int32),
                pltpu.VMEM((2, 2 * half, cols), F32),
                pltpu.VMEM((2, 2 * half, cols), F32),
                pltpu.VMEM((2, 2 * half, cols), F32),
                pltpu.VMEM((2, 2 * half, cols), F32),
                pltpu.VMEM((4, 3 * crow, ccol), F32),
                pltpu.VMEM((slices + 1, 2, 3 * crow, ccol), F32),
                pltpu.VMEM((4 * rows, ccol), F32),
                pltpu.VMEM((2, 3 * crow, ccol), F32),
                pltpu.SemaphoreType.DMA((6,)),
                pltpu.SemaphoreType.DMA((3, 2)),
                pltpu.SemaphoreType.DMA((3, 2)),
                pltpu.SemaphoreType.DMA((cuts, 3, 2)),
                pltpu.SemaphoreType.DMA((3, cuts + 1)),
            ],
            compiler_params=pltpu.CompilerParams(
                collective_id=0, has_side_effects=True, vmem_limit_bytes=32 * 1024 * 1024
            ),
        )(*(
            pltpu.with_memory_space_constraint(given, pltpu.HBM)
            for given in (starts, coarse_prev, zone_ids, materials, current, bounds)
        ))
        return pl.pallas_call(
            finish,
            out_shape=(
                jax.ShapeDtypeStruct(starts.shape, F32),
                jax.ShapeDtypeStruct(coarse_prev.shape, F32),
            ),
            in_specs=[vmem] * 4,
            out_specs=(hbm, hbm),
            scratch_shapes=[
                pltpu.VMEM(starts.shape, F32),
                pltpu.SemaphoreType.DMA((lc + 1,)),
            ],
            compiler_params=pltpu.CompilerParams(vmem_limit_bytes=16 * 1024 * 1024),
        )(fine, new, risen, spread)

    placed = (
        P(("grp", "cuts"), None, ("space", "sub"), None),
        P(("grp", "cuts"), None, ("space", "sub"), None),
        P(("grp", "space", "sub"), None),
        P(),
        P("grp"),
        P(),
    )
    return jax.shard_map(
        local,
        mesh=mesh,
        in_specs=placed,
        out_specs=(
            P(("grp", "cuts"), None, ("space", "sub"), None),
            P(("grp", "cuts"), None, ("space", "sub"), None),
        ),
        check_vma=False,
    )
```
